1024 devices in a mesh: dom: 64 (over z_lo, y), sub: 16 (over x, z_hi, core).
Axes of the slice: x: 4, y: 4, z: 32 (z_hi: 2, z_lo: 16; z = z_hi * 16 + z_lo), core: 2. Of those that a mesh axis runs over, the one named last changes fastest.
Arguments:
- excitation: bfloat16 [64, 512, 4096], P('dom', None, 'sub'), may hold values from -6 to 6
- stiffness: float32 [64, 512, 512], P('dom'), may hold values from -2 to 14, as said below
- traces_prev: float32 [64, 32768], P('dom', 'sub'), may hold values from -6 to 6
- neighbours: int32 [64, 4], P('dom'), may hold values from 0 to 63, as said below
- far_list: int32 [64, 2], P('dom'), may hold values from 0 to 63, as said below
- face_perm: int32 [64, 4, 128], P('dom'), may hold values from 0 to 127, each once within a row
- live_columns: int32 [64], P('dom'), may hold values from 2048 to 4096, as said below
- far_block: bfloat16 [64, 2, 192, 32768], P('dom', None, None, 'sub'), may hold values from -0.03125 to 0.03125
- in_basis: bfloat16 [64, 192, 32768], P('dom', 'sub'), may hold values from -0.4375 to 0.4375
Outputs:
- field: float32 [64, 512, 4096], P('dom', None, 'sub')
- traces_next: float32 [64, 32768], P('dom', 'sub')
The draws below stay inside these ranges and needn't reach their ends.
Inputs may be any that keep to these rules, and one draw needn't show every extreme that they name: `neighbours`: row d names 4 distinct domains other than d; e names d whenever d names e, and each column names every domain once. `far_list`: row d names 2 distinct domains, neither d nor any in row d of neighbours; each column names every domain once. `live_columns`: some domain uses all 4096 columns and some uses exactly half of them. `stiffness`: symmetric in its last two dimensions.
All inputs are finite; a program needn't handle non-finite values.
Results may differ from the reference program's by a relative error of at most 0.0022.
Values may be sent and summed in bfloat16 or wider, within the bound.
A program may use at most 64 MiB of HBM per device.

```python
import math
import jax
import jax.numpy as jnp
from jax import lax

BLK = 512
TRACE = 32768
RANK = 192
TROW = 8
NB = 4
FAR = 2
DEG = 8
PATCH = 128
DOMAINS = 64
COLS = 4096


def domain_cycle(key):
    ordering = jax.random.permutation(key, DOMAINS).astype(jnp.int32)
    position = jnp.argsort(ordering).astype(jnp.int32)
    return (ordering, position)


def draw_neighbours(key, part):
    ordering, position = domain_cycle(key)
    steps = jnp.arange(NB, dtype=jnp.int32)
    offsets = (steps // 2 + 1) * (1 - 2 * (steps % 2))
    target = ordering[(position[:, None] + offsets[None, :]) % DOMAINS]
    return target.astype(jnp.int32)


def draw_far_list(key, part):
    ordering, position = domain_cycle(key)
    offsets = DOMAINS // 2 - FAR // 2 + jnp.arange(FAR, dtype=jnp.int32)
    target = ordering[(position[:, None] + offsets[None, :]) % DOMAINS]
    return target.astype(jnp.int32)


def draw_live_columns(key, part):
    key = jax.random.fold_in(key, 9)
    key_counts, key_picks = jax.random.split(key)
    counts = jax.random.randint(key_counts, (DOMAINS,), COLS // 2, COLS + 1, dtype=jnp.int32)
    picks = jax.random.permutation(key_picks, DOMAINS).astype(jnp.int32)
    indices = jnp.arange(DOMAINS, dtype=jnp.int32)
    counts = jnp.where(indices == picks[0], COLS, counts)
    counts = jnp.where(indices == picks[1], COLS // 2, counts)
    return counts.astype(jnp.int32)


def draw_stiffness(key, part):
    key = jax.random.fold_in(key, 13)
    key_diag, key_noise = jax.random.split(key)
    diagonal_values = jax.random.uniform(key_diag, (DOMAINS, BLK), jnp.float32, 6.0, 14.0)
    noise = jax.random.truncated_normal(key_noise, -3.0, 3.0, (DOMAINS, BLK, BLK), jnp.float32)
    coupling = (noise + jnp.swapaxes(noise, 1, 2)) * (1.6 / math.sqrt(BLK))
    row_index = lax.broadcasted_iota(jnp.int32, (DOMAINS, BLK, BLK), 1)
    col_index = lax.broadcasted_iota(jnp.int32, (DOMAINS, BLK, BLK), 2)
    return jnp.where(row_index == col_index, diagonal_values[:, :, None], coupling).astype(jnp.float32)


def levels(key, dims, cuts, smallest, top_value):
    gain = 1.0
    for axis_at, parts in cuts:
        draws = jax.random.uniform(jax.random.fold_in(jax.random.fold_in(key, 6), axis_at), (parts,), jnp.float32, smallest / len(cuts), top_value / len(cuts))
        gain = gain * jnp.repeat(jnp.exp(draws), dims[axis_at] // parts).reshape((-1,) + (1,) * (len(dims) - 1 - axis_at))
    return gain


def gaussian(stream_key, dims, spread, reach, pieces=(), held_as=jnp.bfloat16):
    gain = levels(stream_key, dims, pieces, -0.22, 0.18) if pieces else 1.0
    array = jax.random.normal(stream_key, dims, jnp.float32) * spread * gain
    return jnp.minimum(jnp.maximum(array, -reach), reach).astype(held_as)


def setup_inputs(seed: int = 0) -> dict:
    streams_of = jax.random.split(jax.random.key(seed), 10)
    return {
        "excitation": gaussian(streams_of[0], (DOMAINS, BLK, COLS), 1.0, 6.0, ((0, 64), (2, 16))),
        "stiffness": draw_stiffness(jax.random.fold_in(streams_of[9], 71), 0),
        "traces_prev": gaussian(streams_of[2], (DOMAINS, TRACE), 1.0, 6.0, ((0, 64), (1, 16)), jnp.float32),
        "neighbours": draw_neighbours(jax.random.fold_in(streams_of[9], 71), 0),
        "far_list": draw_far_list(jax.random.fold_in(streams_of[9], 71), 0),
        "face_perm": jax.vmap(lambda own: jax.random.permutation(own, PATCH))(jax.random.split(streams_of[5], DOMAINS * NB)).reshape((DOMAINS, NB, PATCH)).astype(jnp.int32),
        "live_columns": draw_live_columns(jax.random.fold_in(streams_of[9], 71), 0),
        "far_block": gaussian(streams_of[7], (DOMAINS, FAR, RANK, TRACE), TRACE ** -0.5, 0.03125, ((0, 64), (3, 16))),
        "in_basis": gaussian(streams_of[8], (DOMAINS, RANK, TRACE), RANK ** -0.5, 0.4375, ((0, 64), (1, 16))),
    }


cheb_lower = 0.8
cheb_upper = 24.0
robin_gain = 2.0


def apply_operator(stiff_block, vectors):
    row_index = lax.broadcasted_iota(jnp.int32, vectors.shape, 0)
    boundary = jnp.where(row_index < TROW, robin_gain * vectors, jnp.zeros_like(vectors))
    product = jnp.dot(stiff_block, vectors, precision=lax.Precision.HIGHEST, preferred_element_type=jnp.float32)
    return product + boundary


def chebyshev_smooth(stiff_block, source):
    centre_value = 0.5 * (cheb_upper + cheb_lower)
    half_width = 0.5 * (cheb_upper - cheb_lower)
    sigma_ratio = centre_value / half_width
    rho_previous = 1.0 / sigma_ratio
    solution = jnp.zeros_like(source)
    residue = source
    update = source / centre_value
    for degree_step in range(DEG):
        solution = solution + update
        if degree_step + 1 < DEG:
            residue = residue - apply_operator(stiff_block, update)
            rho_next = 1.0 / (2.0 * sigma_ratio - rho_previous)
            update = (rho_next * rho_previous) * update + (2.0 * rho_next / half_width) * residue
            rho_previous = rho_next
    return solution


def one_domain(traces_all, domain_items):
    excite, stiff_block, near_ids, far_ids, perm_rows, live_count, far_factor, basis_block = domain_items
    near_rows = jnp.take(traces_all, near_ids.astype(jnp.int32), axis=0)
    near_patch = near_rows.reshape(NB, TRACE // PATCH, PATCH)
    moved = jax.vmap(lambda patch_rows, ordering: jnp.take(patch_rows, ordering.astype(jnp.int32), axis=1))(near_patch, perm_rows)
    near_sum = jnp.sum(moved, axis=0).reshape(TRACE)
    far_rows = jnp.take(traces_all, far_ids.astype(jnp.int32), axis=0).astype(jnp.bfloat16)
    coefficient = jnp.einsum("frk,fk->r", far_factor.astype(jnp.float32), far_rows.astype(jnp.float32), precision=lax.Precision.HIGHEST)
    far_sum = jnp.dot(coefficient.astype(jnp.bfloat16), basis_block, preferred_element_type=jnp.float32)
    incoming = (near_sum + far_sum).reshape(COLS, TROW).T
    columns = lax.broadcasted_iota(jnp.int32, (1, COLS), 1)
    live_mask = columns < live_count
    source = excite.astype(jnp.float32) + jnp.pad(incoming, ((0, BLK - TROW), (0, 0)))
    source = jnp.where(live_mask, source, jnp.zeros_like(source))
    field_values = chebyshev_smooth(stiff_block, source)
    outgoing = 2.0 * robin_gain * field_values[:TROW] - incoming
    outgoing = jnp.where(live_mask, outgoing, jnp.zeros_like(outgoing))
    return field_values, outgoing.T.reshape(TRACE)


def reference(excitation, stiffness, traces_prev, neighbours, far_list, face_perm, live_columns, far_block, in_basis):
    def mapped(domain_items):
        return one_domain(traces_prev, domain_items)

    fields, outgoing = lax.map(mapped, (excitation, stiffness, neighbours, far_list, face_perm, live_columns, far_block, in_basis))
    return fields, outgoing
```

```python
import functools
import jax
import jax.numpy as jnp
from jax import lax
from jax.experimental import pallas as pl
from jax.experimental.pallas import tpu as pltpu
from jax.sharding import PartitionSpec as P

MESH = pl.DeviceIdType.MESH
F32 = jnp.float32
BF16 = jnp.bfloat16

BLK = 512
TROW = 8
NB = 4
FAR = 2
DEG = 8
PATCH = 128
RANK = 192
ZN, YN, XN = 16, 4, 4
SUB = 16
OWN = RANK // SUB
QN = 16
COLS = 256
VCOLS = COLS + PATCH

cheb_lower = 0.8
cheb_upper = 24.0
robin_gain = 2.0


def cheb_constants():
    centre = 0.5 * (cheb_upper + cheb_lower)
    half = 0.5 * (cheb_upper - cheb_lower)
    ratio = centre / half
    previous = 1.0 / ratio
    steps = []
    for _ in range(DEG - 1):
        following = 1.0 / (2.0 * ratio - previous)
        steps.append((following * previous, 2.0 * following / half))
        previous = following
    return centre, steps


def split2(values):
    high = values.astype(BF16)
    low = (values - high.astype(F32)).astype(BF16)
    return high, low


def split3(values):
    high = values.astype(BF16)
    rest = values - high.astype(F32)
    middle = rest.astype(BF16)
    low = (rest - middle.astype(F32)).astype(BF16)
    return high, middle, low


def dot_nt(left, right):
    return lax.dot_general(left, right, (((1,), (1,)), ((), ())), preferred_element_type=F32)


def iota(shape, axis):
    return lax.broadcasted_iota(jnp.int32, shape, axis)


def kernel(
    coef_ref,
    exc_hbm,
    stiff_hbm,
    trace_ref,
    neigh_ref,
    farl_ref,
    perm_ref,
    live_ref,
    far_hbm,
    basis_hbm,
    field_ref,
    next_ref,
    exc_v,
    stiff_v,
    far_v,
    basis_v,
    basis_d,
    a3,
    u_v,
    r_v,
    x_v,
    own_t,
    rows_v,
    tab_v,
    sel_v,
    fsend,
    frecv,
    nsend,
    nrecv,
    csend,
    crecv,
    psend,
    precv,
    hsend,
    hrecv,
    t0_v,
    g3_v,
    b3_v,
    lsem,
    zs,
    zr,
    ts,
    tr,
    fs,
    fr,
    ns,
    nr,
    cs,
    cr,
    ps,
    pr,
    hs,
    hr,
):
    dom = lax.axis_index("dom")
    sub = lax.axis_index("sub")
    z, y = dom // YN, dom % YN
    x, h, c = sub // 4, (sub // 2) % 2, sub % 2
    s8 = x * 2 + c

    def z_peer(k):
        return (((z + k) % ZN) * YN + y, sub)

    def y_peer(k):
        return (z * YN + (y + k) % YN, sub)

    def s_peer(k):
        return (dom, (sub + k) % SUB)

    def e_peer(k):
        t = (s8 + k) % 8
        return (dom, (t // 2) * 4 + h * 2 + t % 2)

    across = (dom, x * 4 + (1 - h) * 2 + c)

    barrier = pltpu.get_barrier_semaphore()
    peers = [z_peer(k) for k in range(1, ZN)] + [y_peer(k) for k in range(1, YN)]
    peers += [s_peer(k) for k in range(1, SUB)]
    for peer in peers:
        pl.semaphore_signal(barrier, inc=1, device_id=peer, device_id_type=MESH)

    loads = [
        pltpu.make_async_copy(stiff_hbm, stiff_v, lsem.at[0]),
        pltpu.make_async_copy(exc_hbm, exc_v, lsem.at[1]),
        pltpu.make_async_copy(basis_hbm, basis_v, lsem.at[2]),
        pltpu.make_async_copy(far_hbm, far_v, lsem.at[3]),
    ]
    for load in loads:
        load.start()

    for q in range(QN):
        own_t[q : q + 1, :] = trace_ref[:, q * PATCH : (q + 1) * PATCH]
    rows_v[z] = own_t[...]
    tab_v[0, 0:4, :] = perm_ref[0]
    for j in range(NB):
        tab_v[0, 4 + j : 5 + j, :] = jnp.full((1, PATCH), neigh_ref[0, j], jnp.int32)
    for f in range(FAR):
        tab_v[0, 8 + f : 9 + f, :] = jnp.full((1, PATCH), farl_ref[0, f], jnp.int32)
    tab_v[0, 10:16, :] = jnp.zeros((6, PATCH), jnp.int32)

    loads[0].wait()
    row = iota((BLK, BLK), 0)
    col = iota((BLK, BLK), 1)
    operator = stiff_v[0] + jnp.where((row == col) & (row < TROW), robin_gain, 0.0)
    a_high, a_low = split2(operator)
    a3[:, 0:BLK] = a_high
    a3[:, BLK : 2 * BLK] = a_low
    a3[:, 2 * BLK : 3 * BLK] = a_high

    live = live_ref[0]
    loads[1].wait()
    column = sub * COLS + iota((BLK, COLS), 1)
    r_v[:, 0:COLS] = jnp.where(column < live, exc_v[0].astype(F32), 0.0)
    r_v[:, COLS:] = jnp.where(iota((BLK, PATCH), 0) == iota((BLK, PATCH), 1) % TROW, 1.0, 0.0)
    centre, _ = cheb_constants()
    first = r_v[...] * (1.0 / centre)
    u_v[...] = first
    x_v[...] = first

    def smooth(step, carry):
        u_high, u_low = split2(u_v[...])
        moved = jnp.dot(
            a3[...],
            jnp.concatenate([u_high, u_high, u_low], axis=0),
            preferred_element_type=F32,
        )
        res = r_v[...] - moved
        r_v[...] = res
        following = coef_ref[step, 0] * u_v[...] + coef_ref[step, 1] * res
        u_v[...] = following
        x_v[...] += following
        return carry

    lax.fori_loop(0, 4, smooth, 0)

    pl.semaphore_wait(barrier, len(peers))

    def remote(src, dst, send, recv, peer):
        return pltpu.make_async_remote_copy(
            src_ref=src,
            dst_ref=dst,
            send_sem=send,
            recv_sem=recv,
            device_id=peer,
            device_id_type=MESH,
        )

    z_copies = [
        remote(own_t, rows_v.at[z], zs.at[k], zr.at[k], z_peer(k)) for k in range(1, ZN)
    ]
    t_copies = [
        remote(tab_v.at[0], tab_v.at[YN - k], ts.at[k], tr.at[k], y_peer(k)) for k in range(1, YN)
    ]
    for copy in z_copies:
        copy.start()
    for copy in t_copies:
        copy.start()

    lax.fori_loop(4, DEG - 1, smooth, 0)

    loads[2].wait()
    for r in range(OWN):
        basis_d[r] = basis_v[0, r : r + 1, :].astype(F32).reshape(256, PATCH)

    lane = iota((PATCH, PATCH), 1)
    sublane = iota((PATCH, PATCH), 0)
    g_high, g_low = split2(x_v[:, COLS:])
    g3_v[:, 0:PATCH] = g_high
    g3_v[:, PATCH : 2 * PATCH] = g_high
    g3_v[:, 2 * PATCH :] = g_low
    tiled = jnp.concatenate([x_v[0:TROW, COLS:]] * QN, axis=0)
    gain = jnp.where(lane // TROW == sublane // TROW, (2.0 * robin_gain) * tiled, 0.0)
    b_high, b_low = split2(gain)
    b3_v[:, 0:PATCH] = b_high
    b3_v[:, PATCH : 2 * PATCH] = b_high
    b3_v[:, 2 * PATCH :] = b_low

    pieces = split3((2.0 * robin_gain) * x_v[0:TROW, 0:COLS])
    stacked = jnp.concatenate([piece.astype(F32) for piece in pieces], axis=0).astype(BF16)
    spread = iota((COLS, PATCH), 1) // TROW
    place = iota((COLS, PATCH), 0)
    keep = iota((TROW, PATCH), 0) == iota((TROW, PATCH), 1) % TROW
    for q in range(QN):
        pick = jnp.where(place == q * 16 + spread, 1.0, 0.0).astype(BF16)
        got = jnp.dot(stacked, pick, preferred_element_type=F32)
        got = got[0:8] + got[8:16] + got[16:24]
        t0_v[q : q + 1, :] = jnp.sum(jnp.where(keep, got, 0.0), axis=0, keepdims=True)

    for copy in t_copies:
        copy.wait_recv()
    for t in range(YN):
        for j in range(NB):
            hit = tab_v[t, j : j + 1, :] == sublane
            sel_v[t, j * PATCH : (j + 1) * PATCH, :] = jnp.where(hit, 1.0, 0.0).astype(BF16)

    loads[3].wait()
    for copy in z_copies:
        copy.wait_recv()

    def pick_row(t, entry):
        wanted = jnp.broadcast_to(tab_v[t, entry : entry + 1, :], (QN, PATCH))
        found = jnp.zeros((QN, PATCH), F32)
        for k in range(ZN):
            found = jnp.where(wanted == k * YN + y, rows_v[k], found)
        return found

    f_copies = []
    for t in (2, 1, 3, 0):
        for f in range(FAR):
            fsend[t, f] = pick_row(t, 8 + f)
        if t:
            copy = remote(fsend.at[t], frecv.at[t], fs.at[t], fr.at[t], y_peer(t))
            copy.start()
            f_copies.append(copy)
    n_copies = []
    for t in (2, 1, 3, 0):
        faces = jnp.concatenate([pick_row(t, 4 + j) for j in range(NB)], axis=1)
        three = split3(faces)
        got = jnp.dot(
            jnp.concatenate(three, axis=0), sel_v[t], preferred_element_type=F32
        )
        nsend[t] = (got[0:QN] + got[QN : 2 * QN]) + got[2 * QN :]
        if t:
            copy = remote(nsend.at[t], nrecv.at[t], ns.at[t], nr.at[t], y_peer(t))
            copy.start()
            n_copies.append(copy)

    for copy in f_copies:
        copy.wait_recv()
    partial = jnp.zeros((8, RANK), F32)
    for f in range(FAR):
        remote_rows = ((fsend[0, f] + frecv[1, f]) + (frecv[2, f] + frecv[3, f])).astype(BF16).astype(F32)
        flat = jnp.concatenate([remote_rows[q : q + 1, :] for q in range(QN)], axis=1)
        flat = jnp.broadcast_to(flat, (8, QN * PATCH)).astype(BF16)
        partial += dot_nt(flat, far_v[0, f])
    csend[:, 0:RANK] = partial[0:1, :]
    csend[:, RANK:] = jnp.zeros((1, 256 - RANK), F32)
    crecv[0] = csend[...]
    c_copies = [
        remote(csend, crecv.at[k], cs.at[k], cr.at[k], s_peer(k)) for k in range(1, SUB)
    ]
    for copy in c_copies:
        copy.start()
    for copy in c_copies:
        copy.wait_recv()

    total = crecv[0]
    for k in range(1, SUB):
        total += crecv[k]
    total = total.astype(BF16).astype(F32)
    mine = iota((16, 256), 1) == sub * OWN + iota((16, 256), 0)
    shares = jnp.sum(jnp.where(mine, jnp.broadcast_to(total, (16, 256)), 0.0), axis=1, keepdims=True)
    weights = [jnp.broadcast_to(shares[r : r + 1, :], (QN, PATCH)) for r in range(OWN)]
    for xx in range(XN):
        for hh in range(2):
            for cc in range(2):
                at = (xx * 4 + hh * 2 + cc) * QN
                value = weights[0] * basis_d[0, at : at + QN, :]
                for r in range(1, OWN):
                    value += weights[r] * basis_d[r, at : at + QN, :]
                psend[hh, xx * 2 + cc] = value
    p_copies = [[], []]
    for g in range(2):
        half = 1 - h if g == 0 else h
        for k in range(1, 8):
            copy = remote(
                psend.at[half, (s8 + k) % 8],
                precv.at[g, k],
                ps.at[g, k],
                pr.at[g, k],
                e_peer(k),
            )
            copy.start()
            p_copies[g].append(copy)
    for copy in p_copies[0]:
        copy.wait_recv()
    other = psend[1 - h, s8]
    for k in range(1, 8):
        other += precv[0, k]
    hsend[...] = other
    h_copy = remote(hsend, hrecv, hs.at[0], hr.at[0], across)
    h_copy.start()

    for copy in n_copies:
        copy.wait_recv()
    near = (nsend[0] + nrecv[1]) + (nrecv[2] + nrecv[3])
    for copy in p_copies[1]:
        copy.wait_recv()
    far = psend[h, s8]
    for k in range(1, 8):
        far += precv[1, k]
    h_copy.wait_recv()
    incoming = near + (far + hrecv[...])

    patch_col = sub * COLS + iota((QN, PATCH), 0) * 16 + iota((QN, PATCH), 1) // TROW
    live_trace = patch_col < live
    incoming = jnp.where(live_trace, incoming, 0.0)
    i_high, i_low = split2(incoming)
    i3 = jnp.concatenate([i_high, i_low, i_high], axis=1)
    outgoing = t0_v[...] + dot_nt(i3, b3_v[...]) - incoming
    outgoing = jnp.where(live_trace, outgoing, 0.0)
    for q in range(QN):
        next_ref[:, q * PATCH : (q + 1) * PATCH] = outgoing[q : q + 1, :]

    lanes3 = (iota((16, 3 * PATCH), 1) % PATCH) // TROW == iota((16, 3 * PATCH), 0)
    i3f = i3.astype(F32)
    wide = jnp.concatenate(
        [
            jnp.where(lanes3, jnp.broadcast_to(i3f[q : q + 1, :], (16, 3 * PATCH)), 0.0)
            for q in range(QN)
        ],
        axis=0,
    ).astype(BF16)
    field_ref[0] = x_v[:, 0:COLS] + dot_nt(g3_v[...], wide)

    for copy in z_copies + t_copies + f_copies + n_copies + c_copies + p_copies[0] + p_copies[1]:
        copy.wait_send()
    h_copy.wait_send()


def body(*operands):
    _, steps = cheb_constants()
    constants = jnp.array(steps, F32)
    vmem = pl.BlockSpec(memory_space=pltpu.VMEM)
    smem = pl.BlockSpec(memory_space=pltpu.SMEM)
    hbm = pl.BlockSpec(memory_space=pl.ANY)
    dma = pltpu.SemaphoreType.DMA
    patches = (QN, PATCH)
    return pl.pallas_call(
        kernel,
        out_shape=(
            jax.ShapeDtypeStruct((1, BLK, COLS), F32),
            jax.ShapeDtypeStruct((1, QN * PATCH), F32),
        ),
        in_specs=[smem, hbm, hbm, vmem, smem, smem, vmem, smem, hbm, hbm],
        out_specs=(vmem, vmem),
        scratch_shapes=[
            pltpu.VMEM((1, BLK, COLS), BF16),
            pltpu.VMEM((1, BLK, BLK), F32),
            pltpu.VMEM((1, FAR, RANK, QN * PATCH), BF16),
            pltpu.VMEM((1, OWN, SUB * QN * PATCH), BF16),
            pltpu.VMEM((OWN, SUB * QN, PATCH), F32),
            pltpu.VMEM((BLK, 3 * BLK), BF16),
            pltpu.VMEM((BLK, VCOLS), F32),
            pltpu.VMEM((BLK, VCOLS), F32),
            pltpu.VMEM((BLK, VCOLS), F32),
            pltpu.VMEM(patches, F32),
            pltpu.VMEM((ZN,) + patches, F32),
            pltpu.VMEM((YN, 16, PATCH), jnp.int32),
            pltpu.VMEM((YN, NB * PATCH, PATCH), BF16),
            pltpu.VMEM((YN, FAR) + patches, F32),
            pltpu.VMEM((YN, FAR) + patches, F32),
            pltpu.VMEM((YN,) + patches, F32),
            pltpu.VMEM((YN,) + patches, F32),
            pltpu.VMEM((1, 256), F32),
            pltpu.VMEM((SUB, 1, 256), F32),
            pltpu.VMEM((2, 8) + patches, F32),
            pltpu.VMEM((2, 8) + patches, F32),
            pltpu.VMEM(patches, F32),
            pltpu.VMEM(patches, F32),
            pltpu.VMEM(patches, F32),
            pltpu.VMEM((BLK, 3 * PATCH), BF16),
            pltpu.VMEM((PATCH, 3 * PATCH), BF16),
            dma((4,)),
            dma((ZN,)),
            dma((ZN,)),
            dma((YN,)),
            dma((YN,)),
            dma((YN,)),
            dma((YN,)),
            dma((YN,)),
            dma((YN,)),
            dma((SUB,)),
            dma((SUB,)),
            dma((2, 8)),
            dma((2, 8)),
            dma((1,)),
            dma((1,)),
        ],
        name="robin_sweep",
        compiler_params=pltpu.CompilerParams(
            collective_id=0, has_side_effects=True, vmem_limit_bytes=40 * 1024 * 1024
        ),
    )(constants, *operands)


def solution(mesh):
    placed = (
        P("dom", None, "sub"),
        P("dom", None, None),
        P("dom", "sub"),
        P("dom", None),
        P("dom", None),
        P("dom", None, None),
        P("dom"),
        P("dom", None, None, "sub"),
        P("dom", "sub", None),
    )
    return jax.shard_map(
        body,
        mesh=mesh,
        in_specs=placed,
        out_specs=(P("dom", None, "sub"), P("dom", "sub")),
        check_vma=False,
    )
```

```python
import functools
import jax
import jax.numpy as jnp
from jax import lax
from jax.experimental import pallas as pl
from jax.experimental.pallas import tpu as pltpu
from jax.sharding import PartitionSpec as P

MESH = pl.DeviceIdType.MESH
F32 = jnp.float32
BF16 = jnp.bfloat16

BLK = 512
TROW = 8
NB = 4
FAR = 2
DEG = 8
PATCH = 128
RANK = 192
ZN, YN, XN = 16, 4, 4
SUB = 16
OWN = RANK // SUB
QN = 16
COLS = 256
VCOLS = COLS + PATCH

cheb_lower = 0.8
cheb_upper = 24.0
robin_gain = 2.0


def cheb_constants():
    centre = 0.5 * (cheb_upper + cheb_lower)
    half = 0.5 * (cheb_upper - cheb_lower)
    ratio = centre / half
    previous = 1.0 / ratio
    steps = []
    for _ in range(DEG - 1):
        following = 1.0 / (2.0 * ratio - previous)
        steps.append((following * previous, 2.0 * following / half))
        previous = following
    return centre, steps


def split2(values):
    high = values.astype(BF16)
    low = (values - high.astype(F32)).astype(BF16)
    return high, low


def split3(values):
    high = values.astype(BF16)
    rest = values - high.astype(F32)
    middle = rest.astype(BF16)
    low = (rest - middle.astype(F32)).astype(BF16)
    return high, middle, low


def dot_nt(left, right):
    return lax.dot_general(left, right, (((1,), (1,)), ((), ())), preferred_element_type=F32)


def iota(shape, axis):
    return lax.broadcasted_iota(jnp.int32, shape, axis)


def kernel(
    exc_hbm,
    stiff_hbm,
    trace_hbm,
    neigh_hbm,
    farl_hbm,
    perm_hbm,
    live_hbm,
    far_hbm,
    basis_hbm,
    field_ref,
    next_ref,
    trace_ref,
    neigh_ref,
    farl_ref,
    perm_ref,
    live_ref,
    exc_v,
    stiff_v,
    far_v,
    basis_v,
    basis_d,
    a3,
    u_v,
    r_v,
    x_v,
    own_t,
    rows_v,
    tab_v,
    sel_v,
    fsend,
    frecv,
    nsend,
    nrecv,
    csend,
    crecv,
    psend,
    precv,
    hsend,
    hrecv,
    t0_v,
    g3_v,
    b3_v,
    lsem,
    zs,
    zr,
    ts,
    tr,
    fs,
    fr,
    ns,
    nr,
    cs,
    cr,
    ps,
    pr,
    hs,
    hr,
    side_sem,
    ready_sem,
):
    dom = lax.axis_index("dom")
    sub = lax.axis_index("sub")
    z, y = dom // YN, dom % YN
    x, h, c = sub // 4, (sub // 2) % 2, sub % 2
    s8 = x * 2 + c

    def z_peer(k):
        return (((z + k) % ZN) * YN + y, sub)

    def line_peer(at):
        return (at * YN + y, sub)

    def y_peer(k):
        return (z * YN + (y + k) % YN, sub)

    def s_peer(dx, dh, dc):
        return (dom, ((x + dx) % XN) * 4 + ((h + dh) % 2) * 2 + (c + dc) % 2)

    def e_peer(k):
        t = (s8 + k) % 8
        return (dom, (t // 2) * 4 + h * 2 + t % 2)

    across = (dom, x * 4 + (1 - h) * 2 + c)
    is_end = (z == 0) | (z == ZN - 1)
    touching = ((ZN - 1 - z) * YN + y, x * 4 + (1 - h) * 2 + c)

    def signal(sem, peer):
        pl.semaphore_signal(sem, inc=1, device_id=peer, device_id_type=MESH)

    barrier = pltpu.get_barrier_semaphore()
    peers = [z_peer(k) for k in range(1, ZN)] + [y_peer(k) for k in range(1, YN)]
    peers += [e_peer(k) for k in range(1, 8)]
    for peer in peers:
        signal(barrier, peer)

    @pl.when(is_end)
    def _():
        signal(barrier, touching)

    loads = [
        pltpu.make_async_copy(stiff_hbm, stiff_v, lsem.at[0]),
        pltpu.make_async_copy(exc_hbm, exc_v, lsem.at[1]),
        pltpu.make_async_copy(basis_hbm, basis_v, lsem.at[2]),
        pltpu.make_async_copy(far_hbm, far_v, lsem.at[3]),
    ]
    smalls = [
        pltpu.make_async_copy(trace_hbm, trace_ref, lsem.at[4]),
        pltpu.make_async_copy(perm_hbm, perm_ref, lsem.at[5]),
        pltpu.make_async_copy(neigh_hbm, neigh_ref, lsem.at[6]),
        pltpu.make_async_copy(farl_hbm, farl_ref, lsem.at[7]),
        pltpu.make_async_copy(live_hbm, live_ref, lsem.at[8]),
    ]
    for load in smalls:
        load.start()
    for load in loads:
        load.start()
    for load in smalls:
        load.wait()

    for q in range(QN):
        own_t[q : q + 1, :] = trace_ref[:, q * PATCH : (q + 1) * PATCH]
    rows_v[z] = own_t[...]
    tab_v[0, 0:4, :] = perm_ref[0]
    for j in range(NB):
        tab_v[0, 4 + j : 5 + j, :] = jnp.full((1, PATCH), neigh_ref[0, j], jnp.int32)
    for f in range(FAR):
        tab_v[0, 8 + f : 9 + f, :] = jnp.full((1, PATCH), farl_ref[0, f], jnp.int32)
    tab_v[0, 10:16, :] = jnp.zeros((6, PATCH), jnp.int32)
    live = live_ref[0]
    centre, steps = cheb_constants()

    def remote(src, dst, send, recv, peer):
        return pltpu.make_async_remote_copy(
            src_ref=src,
            dst_ref=dst,
            send_sem=send,
            recv_sem=recv,
            device_id=peer,
            device_id_type=MESH,
        )

    z_copies = [
        remote(own_t, rows_v.at[z], zs.at[k], zr.at[k], z_peer(k))
        for k in (8, 7, 9, 6, 10, 5, 11, 4, 12, 3, 13, 2, 14, 1, 15)
    ]
    t_copies = [
        remote(tab_v.at[0], tab_v.at[YN - k], ts.at[k], tr.at[k], y_peer(k)) for k in range(1, YN)
    ]

    def meet_and_send():
        pl.semaphore_wait(barrier, len(peers) + is_end.astype(jnp.int32))
        for copy in z_copies:
            copy.start()
        for copy in t_copies:
            copy.start()

        @pl.when(is_end)
        def _():
            for k in range(1, 8):
                signal(side_sem, e_peer(k))
            pl.semaphore_wait(side_sem, 7)
            signal(ready_sem, touching)

    early = (h == 0) & (z < ZN // 2)

    def pass_on(chosen):
        @pl.when(is_end & chosen)
        def _():
            pl.semaphore_wait(ready_sem, 1)
            for k in range(1, 8):
                signal(ready_sem, line_peer(jnp.where(z == 0, k, ZN - 1 - k)))

    def local_work():
        smooth_part()
        pass_on(jnp.logical_not(early))
        prepare_part()

    def smooth_part():
        loads[0].wait()
        row = iota((BLK, BLK), 0)
        col = iota((BLK, BLK), 1)
        operator = stiff_v[0] + jnp.where((row == col) & (row < TROW), robin_gain, 0.0)
        a_high, a_low = split2(operator)
        a3[:, 0:BLK] = a_high
        a3[:, BLK : 2 * BLK] = a_low
        a3[:, 2 * BLK : 3 * BLK] = a_high

        loads[1].wait()
        column = sub * COLS + iota((BLK, COLS), 1)
        r_v[:, 0:COLS] = jnp.where(column < live, exc_v[0].astype(F32), 0.0)
        r_v[:, COLS:] = jnp.where(iota((BLK, PATCH), 0) == iota((BLK, PATCH), 1) % TROW, 1.0, 0.0)
        first = r_v[...] * (1.0 / centre)
        u_v[...] = first
        x_v[...] = first

        def smooth(step, carry):
            u_high, u_low = split2(u_v[...])
            moved = jnp.dot(
                a3[...],
                jnp.concatenate([u_high, u_high, u_low], axis=0),
                preferred_element_type=F32,
            )
            res = r_v[...] - moved
            r_v[...] = res
            keep, add = steps[0]
            for at in range(1, DEG - 1):
                keep = jnp.where(step == at, steps[at][0], keep)
                add = jnp.where(step == at, steps[at][1], add)
            following = keep * u_v[...] + add * res
            u_v[...] = following
            x_v[...] += following
            return carry

        lax.fori_loop(0, DEG - 1, smooth, 0)

    lane = iota((PATCH, PATCH), 1)
    sublane = iota((PATCH, PATCH), 0)

    def prepare_part():
        loads[2].wait()
        for r in range(OWN):
            basis_d[r] = basis_v[0, r : r + 1, :].astype(F32).reshape(256, PATCH)

        g_high, g_low = split2(x_v[:, COLS:])
        g3_v[:, 0:PATCH] = g_high
        g3_v[:, PATCH : 2 * PATCH] = g_high
        g3_v[:, 2 * PATCH :] = g_low
        tiled = jnp.concatenate([x_v[0:TROW, COLS:]] * QN, axis=0)
        gain = jnp.where(lane // TROW == sublane // TROW, (2.0 * robin_gain) * tiled, 0.0)
        b_high, b_low = split2(gain)
        b3_v[:, 0:PATCH] = b_high
        b3_v[:, PATCH : 2 * PATCH] = b_high
        b3_v[:, 2 * PATCH :] = b_low

        pieces = split3((2.0 * robin_gain) * x_v[0:TROW, 0:COLS])
        stacked = jnp.concatenate([piece.astype(F32) for piece in pieces], axis=0).astype(BF16)
        spread = iota((COLS, PATCH), 1) // TROW
        place = iota((COLS, PATCH), 0)
        keep = iota((TROW, PATCH), 0) == iota((TROW, PATCH), 1) % TROW
        for q in range(QN):
            pick = jnp.where(place == q * 16 + spread, 1.0, 0.0).astype(BF16)
            got = jnp.dot(stacked, pick, preferred_element_type=F32)
            got = got[0:8] + got[8:16] + got[16:24]
            t0_v[q : q + 1, :] = jnp.sum(jnp.where(keep, got, 0.0), axis=0, keepdims=True)

    def phase(at, carry):
        @pl.when((at == 0) != early)
        def _():
            meet_and_send()

        @pl.when(at == 0)
        def _():
            local_work()

        return carry

    lax.fori_loop(0, 2, phase, 0)

    for copy in t_copies:
        copy.wait_recv()
    for t in range(YN):
        for j in range(NB):
            hit = tab_v[t, j : j + 1, :] == sublane
            sel_v[t, j * PATCH : (j + 1) * PATCH, :] = jnp.where(hit, 1.0, 0.0).astype(BF16)

    loads[3].wait()
    for copy in z_copies:
        copy.wait_recv()

    def pick_row(t, entry):
        wanted = jnp.broadcast_to(tab_v[t, entry : entry + 1, :], (QN, PATCH))
        found = jnp.zeros((QN, PATCH), F32)
        for k in range(ZN):
            found = jnp.where(wanted == k * YN + y, rows_v[k], found)
        return found

    f_copies = []
    for t in (2, 1, 3, 0):
        for f in range(FAR):
            fsend[t, f] = pick_row(t, 8 + f)
        if t:
            copy = remote(fsend.at[t], frecv.at[t], fs.at[t], fr.at[t], y_peer(t))
            copy.start()
            f_copies.append(copy)
    pass_on(early)
    n_copies = []
    for t in (2, 1, 3, 0):
        faces = jnp.concatenate([pick_row(t, 4 + j) for j in range(NB)], axis=1)
        three = split3(faces)
        got = jnp.dot(
            jnp.concatenate(three, axis=0), sel_v[t], preferred_element_type=F32
        )
        nsend[t] = (got[0:QN] + got[QN : 2 * QN]) + got[2 * QN :]
        if t:
            copy = remote(nsend.at[t], nrecv.at[t], ns.at[t], nr.at[t], y_peer(t))
            copy.start()
            n_copies.append(copy)

    for copy in f_copies:
        copy.wait_recv()
    partial = jnp.zeros((8, RANK), F32)
    for f in range(FAR):
        remote_rows = ((fsend[0, f] + frecv[1, f]) + (frecv[2, f] + frecv[3, f])).astype(BF16).astype(F32)
        flat = jnp.concatenate([remote_rows[q : q + 1, :] for q in range(QN)], axis=1)
        flat = jnp.broadcast_to(flat, (8, QN * PATCH)).astype(BF16)
        partial += dot_nt(flat, far_v[0, f])
    csend[:, 0:RANK] = partial[0:1, :]
    csend[:, RANK:] = jnp.zeros((1, 256 - RANK), F32)
    crecv[0] = csend[...]

    @pl.when(jnp.logical_not(is_end))
    def _():
        pl.semaphore_wait(ready_sem, 1)

    c_copies = []
    for dh in (1, 0):
        for dx in (2, 1, 3, 0):
            for dc in (0, 1):
                at = dh * 8 + dx * 2 + dc
                if at:
                    copy = remote(csend, crecv.at[at], cs.at[at], cr.at[at], s_peer(dx, dh, dc))
                    copy.start()
                    c_copies.append(copy)
    for copy in c_copies:
        copy.wait_recv()

    total = crecv[0]
    for k in range(1, SUB):
        total += crecv[k]
    total = total.astype(BF16).astype(F32)
    mine = iota((16, 256), 1) == sub * OWN + iota((16, 256), 0)
    shares = jnp.sum(jnp.where(mine, jnp.broadcast_to(total, (16, 256)), 0.0), axis=1, keepdims=True)
    weights = [jnp.broadcast_to(shares[r : r + 1, :], (QN, PATCH)) for r in range(OWN)]
    for xx in range(XN):
        for hh in range(2):
            for cc in range(2):
                at = (xx * 4 + hh * 2 + cc) * QN
                value = weights[0] * basis_d[0, at : at + QN, :]
                for r in range(1, OWN):
                    value += weights[r] * basis_d[r, at : at + QN, :]
                psend[hh, xx * 2 + cc] = value
    p_copies = [[], []]
    for g in range(2):
        half = 1 - h if g == 0 else h
        for k in range(1, 8):
            copy = remote(
                psend.at[half, (s8 + k) % 8],
                precv.at[g, k],
                ps.at[g, k],
                pr.at[g, k],
                e_peer(k),
            )
            copy.start()
            p_copies[g].append(copy)
    for copy in p_copies[0]:
        copy.wait_recv()
    other = psend[1 - h, s8]
    for k in range(1, 8):
        other += precv[0, k]
    hsend[...] = other
    h_copy = remote(hsend, hrecv, hs.at[0], hr.at[0], across)
    h_copy.start()

    for copy in n_copies:
        copy.wait_recv()
    near = (nsend[0] + nrecv[1]) + (nrecv[2] + nrecv[3])
    for copy in p_copies[1]:
        copy.wait_recv()
    far = psend[h, s8]
    for k in range(1, 8):
        far += precv[1, k]
    h_copy.wait_recv()
    incoming = near + (far + hrecv[...])

    patch_col = sub * COLS + iota((QN, PATCH), 0) * 16 + iota((QN, PATCH), 1) // TROW
    live_trace = patch_col < live
    incoming = jnp.where(live_trace, incoming, 0.0)
    i_high, i_low = split2(incoming)
    i3 = jnp.concatenate([i_high, i_low, i_high], axis=1)
    outgoing = t0_v[...] + dot_nt(i3, b3_v[...]) - incoming
    outgoing = jnp.where(live_trace, outgoing, 0.0)
    for q in range(QN):
        next_ref[:, q * PATCH : (q + 1) * PATCH] = outgoing[q : q + 1, :]

    lanes3 = (iota((16, 3 * PATCH), 1) % PATCH) // TROW == iota((16, 3 * PATCH), 0)
    i3f = i3.astype(F32)
    wide = jnp.concatenate(
        [
            jnp.where(lanes3, jnp.broadcast_to(i3f[q : q + 1, :], (16, 3 * PATCH)), 0.0)
            for q in range(QN)
        ],
        axis=0,
    ).astype(BF16)
    field_ref[0] = x_v[:, 0:COLS] + dot_nt(g3_v[...], wide)

    for copy in z_copies + t_copies + f_copies + n_copies + c_copies + p_copies[0] + p_copies[1]:
        copy.wait_send()
    h_copy.wait_send()


def body(*operands):
    vmem = pl.BlockSpec(memory_space=pltpu.VMEM)
    hbm = pl.BlockSpec(memory_space=pltpu.HBM)
    dma = pltpu.SemaphoreType.DMA
    patches = (QN, PATCH)
    return pl.pallas_call(
        kernel,
        out_shape=(
            jax.ShapeDtypeStruct((1, BLK, COLS), F32),
            jax.ShapeDtypeStruct((1, QN * PATCH), F32),
        ),
        in_specs=[hbm] * 9,
        out_specs=(vmem, vmem),
        scratch_shapes=[
            pltpu.VMEM((1, QN * PATCH), F32),
            pltpu.SMEM((1, NB), jnp.int32),
            pltpu.SMEM((1, FAR), jnp.int32),
            pltpu.VMEM((1, NB, PATCH), jnp.int32),
            pltpu.SMEM((1,), jnp.int32),
            pltpu.VMEM((1, BLK, COLS), BF16),
            pltpu.VMEM((1, BLK, BLK), F32),
            pltpu.VMEM((1, FAR, RANK, QN * PATCH), BF16),
            pltpu.VMEM((1, OWN, SUB * QN * PATCH), BF16),
            pltpu.VMEM((OWN, SUB * QN, PATCH), F32),
            pltpu.VMEM((BLK, 3 * BLK), BF16),
            pltpu.VMEM((BLK, VCOLS), F32),
            pltpu.VMEM((BLK, VCOLS), F32),
            pltpu.VMEM((BLK, VCOLS), F32),
            pltpu.VMEM(patches, F32),
            pltpu.VMEM((ZN,) + patches, F32),
            pltpu.VMEM((YN, 16, PATCH), jnp.int32),
            pltpu.VMEM((YN, NB * PATCH, PATCH), BF16),
            pltpu.VMEM((YN, FAR) + patches, F32),
            pltpu.VMEM((YN, FAR) + patches, F32),
            pltpu.VMEM((YN,) + patches, F32),
            pltpu.VMEM((YN,) + patches, F32),
            pltpu.VMEM((1, 256), F32),
            pltpu.VMEM((SUB, 1, 256), F32),
            pltpu.VMEM((2, 8) + patches, F32),
            pltpu.VMEM((2, 8) + patches, F32),
            pltpu.VMEM(patches, F32),
            pltpu.VMEM(patches, F32),
            pltpu.VMEM(patches, F32),
            pltpu.VMEM((BLK, 3 * PATCH), BF16),
            pltpu.VMEM((PATCH, 3 * PATCH), BF16),
            dma((9,)),
            dma((ZN,)),
            dma((ZN,)),
            dma((YN,)),
            dma((YN,)),
            dma((YN,)),
            dma((YN,)),
            dma((YN,)),
            dma((YN,)),
            dma((SUB,)),
            dma((SUB,)),
            dma((2, 8)),
            dma((2, 8)),
            dma((1,)),
            dma((1,)),
            pltpu.SemaphoreType.REGULAR,
            pltpu.SemaphoreType.REGULAR,
        ],
        name="robin_sweep",
        compiler_params=pltpu.CompilerParams(
            collective_id=0, has_side_effects=True, vmem_limit_bytes=60 * 1024 * 1024
        ),
    )(*operands)


def solution(mesh):
    placed = (
        P("dom", None, "sub"),
        P("dom", None, None),
        P("dom", "sub"),
        P("dom", None),
        P("dom", None),
        P("dom", None, None),
        P("dom"),
        P("dom", None, None, "sub"),
        P("dom", "sub", None),
    )
    return jax.shard_map(
        body,
        mesh=mesh,
        in_specs=placed,
        out_specs=(P("dom", None, "sub"), P("dom", "sub")),
        check_vma=False,
    )
```

```python
import functools
import jax
import jax.numpy as jnp
from jax import lax
from jax.experimental import pallas as pl
from jax.experimental.pallas import tpu as pltpu
from jax.sharding import PartitionSpec as P

MESH = pl.DeviceIdType.MESH
F32 = jnp.float32
BF16 = jnp.bfloat16

BLK = 512
TROW = 8
NB = 4
FAR = 2
DEG = 8
PATCH = 128
RANK = 192
ZN, YN, XN = 16, 4, 4
SUB = 16
OWN = RANK // SUB
QN = 16
COLS = 256
VCOLS = COLS + PATCH

cheb_lower = 0.8
cheb_upper = 24.0
robin_gain = 2.0


def cheb_constants():
    centre = 0.5 * (cheb_upper + cheb_lower)
    half = 0.5 * (cheb_upper - cheb_lower)
    ratio = centre / half
    previous = 1.0 / ratio
    steps = []
    for _ in range(DEG - 1):
        following = 1.0 / (2.0 * ratio - previous)
        steps.append((following * previous, 2.0 * following / half))
        previous = following
    return centre, steps


def split2(values):
    high = values.astype(BF16)
    low = (values - high.astype(F32)).astype(BF16)
    return high, low


def split3(values):
    high = values.astype(BF16)
    rest = values - high.astype(F32)
    middle = rest.astype(BF16)
    low = (rest - middle.astype(F32)).astype(BF16)
    return high, middle, low


def dot_nt(left, right):
    return lax.dot_general(left, right, (((1,), (1,)), ((), ())), preferred_element_type=F32)


def iota(shape, axis):
    return lax.broadcasted_iota(jnp.int32, shape, axis)


def kernel(
    exc_hbm,
    stiff_hbm,
    trace_hbm,
    neigh_hbm,
    farl_hbm,
    perm_hbm,
    live_hbm,
    far_hbm,
    basis_hbm,
    field_ref,
    next_ref,
    trace_ref,
    neigh_ref,
    farl_ref,
    perm_ref,
    live_ref,
    exc_v,
    stiff_v,
    far_v,
    basis_v,
    basis_d,
    a3,
    u_v,
    r_v,
    x_v,
    own_hi,
    own_lo,
    rows_hi,
    rows_lo,
    tab_v,
    sel_v,
    fsend,
    frecv,
    nsend,
    nrecv,
    csend,
    crecv,
    psend,
    precv,
    hsend,
    hrecv,
    t0_v,
    g3_v,
    b3_v,
    lsem,
    zs,
    zr,
    ts,
    tr,
    fs,
    fr,
    ns,
    nr,
    cs,
    cr,
    ps,
    pr,
    hs,
    hr,
    side_sem,
    ready_sem,
    hub_sem,
    up_sem,
):
    dom = lax.axis_index("dom")
    sub = lax.axis_index("sub")
    z, y = dom // YN, dom % YN
    x, h, c = sub // 4, (sub // 2) % 2, sub % 2
    s8 = x * 2 + c

    def z_peer(k):
        return (((z + k) % ZN) * YN + y, sub)

    def line_peer(at):
        return (at * YN + y, sub)

    def y_peer(k):
        return (z * YN + (y + k) % YN, sub)

    def s_peer(dx, dh, dc):
        return (dom, ((x + dx) % XN) * 4 + ((h + dh) % 2) * 2 + (c + dc) % 2)

    def e_peer(k):
        t = (s8 + k) % 8
        return (dom, (t // 2) * 4 + h * 2 + t % 2)

    across = (dom, x * 4 + (1 - h) * 2 + c)
    first, second = h == 0, h == 1
    is_end = (z == 0) | (z == ZN - 1)
    touching = ((ZN - 1 - z) * YN + y, x * 4 + (1 - h) * 2 + c)
    direct = second | (z < ZN // 2)
    hub = first & (z == ZN // 2 - 1)

    turned = jnp.where(z < ZN // 2, ZN - 1 - z, z)

    def line_at(i):
        place = i + (i >= turned).astype(jnp.int32)
        return jnp.where(z < ZN // 2, ZN - 1 - place, place)

    def signal(sem, peer):
        pl.semaphore_signal(sem, inc=1, device_id=peer, device_id_type=MESH)

    smalls = [
        pltpu.make_async_copy(trace_hbm, trace_ref, lsem.at[4]),
        pltpu.make_async_copy(perm_hbm, perm_ref, lsem.at[5]),
        pltpu.make_async_copy(neigh_hbm, neigh_ref, lsem.at[6]),
        pltpu.make_async_copy(farl_hbm, farl_ref, lsem.at[7]),
        pltpu.make_async_copy(live_hbm, live_ref, lsem.at[8]),
    ]
    for load in smalls:
        load.start()

    barrier = pltpu.get_barrier_semaphore()
    side_peers = [y_peer(k) for k in range(1, YN)] + [e_peer(k) for k in range(1, 8)]
    for i in range(ZN - 1):
        at = line_at(i)

        @pl.when(second | (at > z))
        def _():
            signal(barrier, line_peer(at))

    @pl.when(direct)
    def _():
        for peer in side_peers:
            signal(barrier, peer)

    @pl.when(first & is_end)
    def _():
        signal(barrier, touching)

    loads = [
        pltpu.make_async_copy(stiff_hbm, stiff_v, lsem.at[0]),
        pltpu.make_async_copy(exc_hbm, exc_v, lsem.at[1]),
        pltpu.make_async_copy(basis_hbm, basis_v, lsem.at[2]),
        pltpu.make_async_copy(far_hbm, far_v, lsem.at[3]),
    ]
    for load in loads:
        load.start()
    for load in smalls:
        load.wait()

    own = jnp.concatenate([trace_ref[:, q * PATCH : (q + 1) * PATCH] for q in range(QN)], axis=0)
    high, low = split2(own)
    own_hi[...] = high
    own_lo[...] = low
    rows_hi[z] = high
    rows_lo[z] = low
    tab_v[0, 0:4, :] = perm_ref[0]
    for j in range(NB):
        tab_v[0, 4 + j : 5 + j, :] = jnp.full((1, PATCH), neigh_ref[0, j], jnp.int32)
    for f in range(FAR):
        tab_v[0, 8 + f : 9 + f, :] = jnp.full((1, PATCH), farl_ref[0, f], jnp.int32)
    tab_v[0, 10:16, :] = jnp.zeros((6, PATCH), jnp.int32)
    live = live_ref[0]
    centre, steps = cheb_constants()

    def remote(src, dst, send, recv, peer):
        return pltpu.make_async_remote_copy(
            src_ref=src,
            dst_ref=dst,
            send_sem=send,
            recv_sem=recv,
            device_id=peer,
            device_id_type=MESH,
        )

    def z_start(own_ref, rows_ref, part, chosen):
        for i in range(ZN - 1):
            at = line_at(i)

            @pl.when(chosen(at))
            def _():
                remote(
                    own_ref, rows_ref.at[z], zs.at[part, at], zr.at[part, z], line_peer(at)
                ).start()

    def z_wait(own_ref, rows_ref, part):
        for i in range(ZN - 1):
            at = line_at(i)
            remote(own_ref, rows_ref.at[at], zs.at[part, at], zr.at[part, at], line_peer(at)).wait_recv()

    def z_sent(own_ref, rows_ref, part):
        for i in range(ZN - 1):
            at = line_at(i)
            remote(own_ref, rows_ref.at[z], zs.at[part, at], zr.at[part, z], line_peer(at)).wait_send()

    t_copies = [
        remote(tab_v.at[0], tab_v.at[YN - k], ts.at[k], tr.at[k], y_peer(k)) for k in range(1, YN)
    ]

    def meet_and_send():
        expected = jnp.where(second, ZN - 1, z) + len(side_peers) * direct.astype(jnp.int32)
        pl.semaphore_wait(barrier, expected + (second & is_end).astype(jnp.int32))

        @pl.when(second & is_end)
        def _():
            for k in range(1, 8):
                signal(side_sem, e_peer(k))

        z_start(own_hi, rows_hi, 0, lambda at: second | (at < z))
        for i in range(ZN - 1):
            at = line_at(i)

            @pl.when(first & (at < z))
            def _():
                signal(up_sem, line_peer(at))

        @pl.when(direct)
        def _():
            for copy in t_copies:
                copy.start()

        @pl.when(second & is_end)
        def _():
            pl.semaphore_wait(side_sem, 7)
            signal(ready_sem, touching)

    def answer_line():
        @pl.when(z < ZN - 1)
        def _():
            pl.semaphore_wait(up_sem, ZN - 1 - z)

        @pl.when(z == 0)
        def _():
            for k in range(1, 8):
                signal(side_sem, e_peer(k))

        @pl.when(hub)
        def _():
            for peer in side_peers:
                signal(side_sem, peer)

        z_start(own_hi, rows_hi, 0, lambda at: at > z)

        @pl.when(hub)
        def _():
            pl.semaphore_wait(side_sem, len(side_peers))
            for at in range(ZN // 2, ZN):
                signal(hub_sem, line_peer(at))

    def pass_on():
        for k in range(1, 8):
            signal(ready_sem, line_peer(jnp.where(z == 0, k, ZN - 1 - k)))

    def return_word():
        pl.semaphore_wait(ready_sem, 1)
        signal(ready_sem, touching)
        pass_on()

    def local_work():
        smooth_part()
        prepare_part()

    def smooth_part():
        loads[0].wait()
        row = iota((BLK, BLK), 0)
        col = iota((BLK, BLK), 1)
        operator = stiff_v[0] + jnp.where((row == col) & (row < TROW), robin_gain, 0.0)
        a_high, a_low = split2(operator)
        a3[:, 0:BLK] = a_high
        a3[:, BLK : 2 * BLK] = a_low
        a3[:, 2 * BLK : 3 * BLK] = a_high

        loads[1].wait()
        column = sub * COLS + iota((BLK, COLS), 1)
        r_v[:, 0:COLS] = jnp.where(column < live, exc_v[0].astype(F32), 0.0)
        r_v[:, COLS:] = jnp.where(iota((BLK, PATCH), 0) == iota((BLK, PATCH), 1) % TROW, 1.0, 0.0)
        first = r_v[...] * (1.0 / centre)
        u_v[...] = first
        x_v[...] = first

        def smooth(step, carry):
            u_high, u_low = split2(u_v[...])
            moved = jnp.dot(
                a3[...],
                jnp.concatenate([u_high, u_high, u_low], axis=0),
                preferred_element_type=F32,
            )
            res = r_v[...] - moved
            r_v[...] = res
            keep, add = steps[0]
            for at in range(1, DEG - 1):
                keep = jnp.where(step == at, steps[at][0], keep)
                add = jnp.where(step == at, steps[at][1], add)
            following = keep * u_v[...] + add * res
            u_v[...] = following
            x_v[...] += following
            return carry

        lax.fori_loop(0, DEG - 1, smooth, 0)

    lane = iota((PATCH, PATCH), 1)
    sublane = iota((PATCH, PATCH), 0)

    def prepare_part():
        loads[2].wait()
        for r in range(OWN):
            basis_d[r] = basis_v[0, r : r + 1, :].astype(F32).reshape(256, PATCH)

        g_high, g_low = split2(x_v[:, COLS:])
        g3_v[:, 0:PATCH] = g_high
        g3_v[:, PATCH : 2 * PATCH] = g_high
        g3_v[:, 2 * PATCH :] = g_low
        tiled = jnp.concatenate([x_v[0:TROW, COLS:]] * QN, axis=0)
        gain = jnp.where(lane // TROW == sublane // TROW, (2.0 * robin_gain) * tiled, 0.0)
        b_high, b_low = split2(gain)
        b3_v[:, 0:PATCH] = b_high
        b3_v[:, PATCH : 2 * PATCH] = b_high
        b3_v[:, 2 * PATCH :] = b_low

        pieces = split3((2.0 * robin_gain) * x_v[0:TROW, 0:COLS])
        stacked = jnp.concatenate([piece.astype(F32) for piece in pieces], axis=0).astype(BF16)
        spread = iota((COLS, PATCH), 1) // TROW
        place = iota((COLS, PATCH), 0)
        keep = iota((TROW, PATCH), 0) == iota((TROW, PATCH), 1) % TROW
        for q in range(QN):
            pick = jnp.where(place == q * 16 + spread, 1.0, 0.0).astype(BF16)
            got = jnp.dot(stacked, pick, preferred_element_type=F32)
            got = got[0:8] + got[8:16] + got[16:24]
            t0_v[q : q + 1, :] = jnp.sum(jnp.where(keep, got, 0.0), axis=0, keepdims=True)

    def phase(at, carry):
        @pl.when((at == 0) == first)
        def _():
            meet_and_send()

        @pl.when(at == 0)
        def _():
            local_work()

        return carry

    lax.fori_loop(0, 2, phase, 0)

    @pl.when(first)
    def _():
        answer_line()

    @pl.when(jnp.logical_not(direct))
    def _():
        pl.semaphore_wait(hub_sem, 1)
        for copy in t_copies:
            copy.start()

    @pl.when(first & (z == ZN - 1))
    def _():
        return_word()

    @pl.when(second & is_end)
    def _():
        pl.semaphore_wait(ready_sem, 1)
        pass_on()

    for copy in t_copies:
        copy.wait_recv()
    for t in range(YN):
        for j in range(NB):
            hit = tab_v[t, j : j + 1, :] == sublane
            sel_v[t, j * PATCH : (j + 1) * PATCH, :] = jnp.where(hit, 1.0, 0.0).astype(BF16)

    loads[3].wait()
    z_wait(own_hi, rows_hi, 0)

    def pick_row(t, entry, rows):
        wanted = jnp.broadcast_to(tab_v[t, entry : entry + 1, :], (QN, PATCH))
        found = jnp.zeros((QN, PATCH), F32)
        for k in range(ZN):
            found = jnp.where(wanted == k * YN + y, rows[k], found)
        return found

    f_copies = []
    high_rows = [rows_hi[k].astype(F32) for k in range(ZN)]
    for t in (2, 1, 3, 0):
        for f in range(FAR):
            fsend[t, f] = pick_row(t, 8 + f, high_rows).astype(BF16)
        if t:
            copy = remote(fsend.at[t], frecv.at[t], fs.at[t], fr.at[t], y_peer(t))
            copy.start()
            f_copies.append(copy)
    z_start(own_lo, rows_lo, 1, lambda at: at >= 0)

    @pl.when(first & (z == 0))
    def _():
        pl.semaphore_wait(side_sem, 7)
        return_word()


    for copy in f_copies:
        copy.wait_recv()
    partial = jnp.zeros((8, RANK), F32)
    for f in range(FAR):
        remote_rows = fsend[0, f].astype(F32)
        for t in range(1, YN):
            remote_rows += frecv[t, f].astype(F32)
        flat = jnp.concatenate([remote_rows[q : q + 1, :] for q in range(QN)], axis=1)
        flat = jnp.broadcast_to(flat, (8, QN * PATCH)).astype(BF16)
        partial += dot_nt(flat, far_v[0, f])
    csend[:, 0:RANK] = partial[0:1, :]
    csend[:, RANK:] = jnp.zeros((1, 256 - RANK), F32)
    crecv[0] = csend[...]

    @pl.when(jnp.logical_not(is_end))
    def _():
        pl.semaphore_wait(ready_sem, 1)

    c_copies = []
    for dh in (1, 0):
        for dx in (2, 1, 3, 0):
            for dc in (0, 1):
                at = dh * 8 + dx * 2 + dc
                if at:
                    copy = remote(csend, crecv.at[at], cs.at[at], cr.at[at], s_peer(dx, dh, dc))
                    copy.start()
                    c_copies.append(copy)
    for copy in c_copies:
        copy.wait_recv()

    total = crecv[0]
    for k in range(1, SUB):
        total += crecv[k]
    total = total.astype(BF16).astype(F32)
    mine = iota((16, 256), 1) == sub * OWN + iota((16, 256), 0)
    shares = jnp.sum(jnp.where(mine, jnp.broadcast_to(total, (16, 256)), 0.0), axis=1, keepdims=True)
    weights = [jnp.broadcast_to(shares[r : r + 1, :], (QN, PATCH)) for r in range(OWN)]
    for xx in range(XN):
        for hh in range(2):
            for cc in range(2):
                at = (xx * 4 + hh * 2 + cc) * QN
                value = weights[0] * basis_d[0, at : at + QN, :]
                for r in range(1, OWN):
                    value += weights[r] * basis_d[r, at : at + QN, :]
                psend[hh, xx * 2 + cc] = value
    p_copies = [[], []]
    for g in range(2):
        half = 1 - h if g == 0 else h
        for k in range(1, 8):
            copy = remote(
                psend.at[half, (s8 + k) % 8],
                precv.at[g, k],
                ps.at[g, k],
                pr.at[g, k],
                e_peer(k),
            )
            copy.start()
            p_copies[g].append(copy)
    for copy in p_copies[0]:
        copy.wait_recv()
    other = psend[1 - h, s8]
    for k in range(1, 8):
        other += precv[0, k]
    hsend[...] = other
    h_copy = remote(hsend, hrecv, hs.at[0], hr.at[0], across)
    h_copy.start()

    z_wait(own_lo, rows_lo, 1)
    full_rows = [rows_hi[k].astype(F32) + rows_lo[k].astype(F32) for k in range(ZN)]
    n_copies = []
    for t in (2, 1, 3, 0):
        faces = jnp.concatenate([pick_row(t, 4 + j, full_rows) for j in range(NB)], axis=1)
        got = jnp.dot(
            jnp.concatenate(split2(faces), axis=0), sel_v[t], preferred_element_type=F32
        )
        nsend[t] = got[0:QN] + got[QN:]
        if t:
            copy = remote(nsend.at[t], nrecv.at[t], ns.at[t], nr.at[t], y_peer(t))
            copy.start()
            n_copies.append(copy)

    for copy in n_copies:
        copy.wait_recv()
    near = (nsend[0] + nrecv[1]) + (nrecv[2] + nrecv[3])
    for copy in p_copies[1]:
        copy.wait_recv()
    far = psend[h, s8]
    for k in range(1, 8):
        far += precv[1, k]
    h_copy.wait_recv()
    incoming = near + (far + hrecv[...])

    patch_col = sub * COLS + iota((QN, PATCH), 0) * 16 + iota((QN, PATCH), 1) // TROW
    live_trace = patch_col < live
    incoming = jnp.where(live_trace, incoming, 0.0)
    i_high, i_low = split2(incoming)
    i3 = jnp.concatenate([i_high, i_low, i_high], axis=1)
    outgoing = t0_v[...] + dot_nt(i3, b3_v[...]) - incoming
    outgoing = jnp.where(live_trace, outgoing, 0.0)
    for q in range(QN):
        next_ref[:, q * PATCH : (q + 1) * PATCH] = outgoing[q : q + 1, :]

    lanes3 = (iota((16, 3 * PATCH), 1) % PATCH) // TROW == iota((16, 3 * PATCH), 0)
    i3f = i3.astype(F32)
    wide = jnp.concatenate(
        [
            jnp.where(lanes3, jnp.broadcast_to(i3f[q : q + 1, :], (16, 3 * PATCH)), 0.0)
            for q in range(QN)
        ],
        axis=0,
    ).astype(BF16)
    field_ref[0] = x_v[:, 0:COLS] + dot_nt(g3_v[...], wide)

    z_sent(own_hi, rows_hi, 0)
    z_sent(own_lo, rows_lo, 1)
    for copy in t_copies + f_copies + n_copies + c_copies + p_copies[0] + p_copies[1]:
        copy.wait_send()
    h_copy.wait_send()


def body(*operands):
    vmem = pl.BlockSpec(memory_space=pltpu.VMEM)
    hbm = pl.BlockSpec(memory_space=pltpu.HBM)
    dma = pltpu.SemaphoreType.DMA
    patches = (QN, PATCH)
    return pl.pallas_call(
        kernel,
        out_shape=(
            jax.ShapeDtypeStruct((1, BLK, COLS), F32),
            jax.ShapeDtypeStruct((1, QN * PATCH), F32),
        ),
        in_specs=[hbm] * 9,
        out_specs=(vmem, vmem),
        scratch_shapes=[
            pltpu.VMEM((1, QN * PATCH), F32),
            pltpu.SMEM((1, NB), jnp.int32),
            pltpu.SMEM((1, FAR), jnp.int32),
            pltpu.VMEM((1, NB, PATCH), jnp.int32),
            pltpu.SMEM((1,), jnp.int32),
            pltpu.VMEM((1, BLK, COLS), BF16),
            pltpu.VMEM((1, BLK, BLK), F32),
            pltpu.VMEM((1, FAR, RANK, QN * PATCH), BF16),
            pltpu.VMEM((1, OWN, SUB * QN * PATCH), BF16),
            pltpu.VMEM((OWN, SUB * QN, PATCH), F32),
            pltpu.VMEM((BLK, 3 * BLK), BF16),
            pltpu.VMEM((BLK, VCOLS), F32),
            pltpu.VMEM((BLK, VCOLS), F32),
            pltpu.VMEM((BLK, VCOLS), F32),
            pltpu.VMEM(patches, BF16),
            pltpu.VMEM(patches, BF16),
            pltpu.VMEM((ZN,) + patches, BF16),
            pltpu.VMEM((ZN,) + patches, BF16),
            pltpu.VMEM((YN, 16, PATCH), jnp.int32),
            pltpu.VMEM((YN, NB * PATCH, PATCH), BF16),
            pltpu.VMEM((YN, FAR) + patches, BF16),
            pltpu.VMEM((YN, FAR) + patches, BF16),
            pltpu.VMEM((YN,) + patches, F32),
            pltpu.VMEM((YN,) + patches, F32),
            pltpu.VMEM((1, 256), F32),
            pltpu.VMEM((SUB, 1, 256), F32),
            pltpu.VMEM((2, 8) + patches, F32),
            pltpu.VMEM((2, 8) + patches, F32),
            pltpu.VMEM(patches, F32),
            pltpu.VMEM(patches, F32),
            pltpu.VMEM(patches, F32),
            pltpu.VMEM((BLK, 3 * PATCH), BF16),
            pltpu.VMEM((PATCH, 3 * PATCH), BF16),
            dma((9,)),
            dma((2, ZN)),
            dma((2, ZN)),
            dma((YN,)),
            dma((YN,)),
            dma((YN,)),
            dma((YN,)),
            dma((YN,)),
            dma((YN,)),
            dma((SUB,)),
            dma((SUB,)),
            dma((2, 8)),
            dma((2, 8)),
            dma((1,)),
            dma((1,)),
            pltpu.SemaphoreType.REGULAR,
            pltpu.SemaphoreType.REGULAR,
            pltpu.SemaphoreType.REGULAR,
            pltpu.SemaphoreType.REGULAR,
        ],
        name="robin_sweep",
        compiler_params=pltpu.CompilerParams(
            collective_id=0, has_side_effects=True, vmem_limit_bytes=40 * 1024 * 1024
        ),
    )(*[o if o.ndim == 1 else pltpu.with_memory_space_constraint(o, pltpu.HBM) for o in operands])


def solution(mesh):
    placed = (
        P("dom", None, "sub"),
        P("dom", None, None),
        P("dom", "sub"),
        P("dom", None),
        P("dom", None),
        P("dom", None, None),
        P("dom"),
        P("dom", None, None, "sub"),
        P("dom", "sub", None),
    )
    return jax.shard_map(
        body,
        mesh=mesh,
        in_specs=placed,
        out_specs=(P("dom", None, "sub"), P("dom", "sub")),
        check_vma=False,
    )
```

```python
import functools
import jax
import jax.numpy as jnp
from jax import lax
from jax.experimental import pallas as pl
from jax.experimental.pallas import tpu as pltpu
from jax.sharding import PartitionSpec as P

MESH = pl.DeviceIdType.MESH
F32 = jnp.float32
BF16 = jnp.bfloat16

BLK = 512
TROW = 8
NB = 4
FAR = 2
DEG = 8
PATCH = 128
RANK = 192
ZN, YN, XN = 16, 4, 4
SUB = 16
OWN = RANK // SUB
QN = 16
COLS = 256
VCOLS = COLS + PATCH

cheb_lower = 0.8
cheb_upper = 24.0
robin_gain = 2.0


def cheb_constants():
    centre = 0.5 * (cheb_upper + cheb_lower)
    half = 0.5 * (cheb_upper - cheb_lower)
    ratio = centre / half
    previous = 1.0 / ratio
    steps = []
    for _ in range(DEG - 1):
        following = 1.0 / (2.0 * ratio - previous)
        steps.append((following * previous, 2.0 * following / half))
        previous = following
    return centre, steps


def split2(values):
    high = values.astype(BF16)
    low = (values - high.astype(F32)).astype(BF16)
    return high, low


def split3(values):
    high = values.astype(BF16)
    rest = values - high.astype(F32)
    middle = rest.astype(BF16)
    low = (rest - middle.astype(F32)).astype(BF16)
    return high, middle, low


def dot_nt(left, right):
    return lax.dot_general(left, right, (((1,), (1,)), ((), ())), preferred_element_type=F32)


def iota(shape, axis):
    return lax.broadcasted_iota(jnp.int32, shape, axis)


def kernel(
    exc_hbm,
    stiff_hbm,
    trace_hbm,
    neigh_hbm,
    farl_hbm,
    perm_hbm,
    live_hbm,
    far_hbm,
    basis_hbm,
    field_ref,
    next_ref,
    trace_ref,
    neigh_ref,
    farl_ref,
    perm_ref,
    live_ref,
    exc_v,
    stiff_v,
    far_v,
    basis_v,
    basis_d,
    a3,
    u_v,
    r_v,
    x_v,
    own_hi,
    own_lo,
    rows_hi,
    rows_lo,
    tab_v,
    sel_v,
    fsend,
    frecv,
    nsend,
    nrecv,
    csend,
    crecv,
    psend,
    precv,
    psend_b,
    precv_b,
    t0_v,
    g3_v,
    b3_v,
    lsem,
    zs,
    zr,
    ts,
    tr,
    fs,
    fr,
    ns,
    nr,
    cs,
    cr,
    ps,
    pr,
    hs,
    hr,
    side_sem,
    ready_sem,
    hub_sem,
    up_sem,
):
    dom = lax.axis_index("dom")
    sub = lax.axis_index("sub")
    z, y = dom // YN, dom % YN
    x, h, c = sub // 4, (sub // 2) % 2, sub % 2
    s8 = x * 2 + c

    def z_peer(k):
        return (((z + k) % ZN) * YN + y, sub)

    def line_peer(at):
        return (at * YN + y, sub)

    def y_peer(k):
        return (z * YN + (y + k) % YN, sub)

    def s_peer(dx, dh, dc):
        return (dom, ((x + dx) % XN) * 4 + ((h + dh) % 2) * 2 + (c + dc) % 2)

    def e_peer(k):
        t = (s8 + k) % 8
        return (dom, (t // 2) * 4 + h * 2 + t % 2)

    first, second = h == 0, h == 1
    is_end = (z == 0) | (z == ZN - 1)
    touching = ((ZN - 1 - z) * YN + y, x * 4 + (1 - h) * 2 + c)
    direct = second | (z < ZN // 2)
    hub = first & (z == ZN // 2 - 1)

    special = first & (y == 0) & (x == 0) & (c == 0)
    beyond = special & (z >= ZN // 2)
    origin = special & (z == 0)
    relay = special & (z == 1)

    turned = jnp.where(z < ZN // 2, ZN - 1 - z, z)

    def line_at(i):
        place = i + (i >= turned).astype(jnp.int32)
        return jnp.where(z < ZN // 2, ZN - 1 - place, place)

    def signal(sem, peer):
        pl.semaphore_signal(sem, inc=1, device_id=peer, device_id_type=MESH)

    smalls = [
        pltpu.make_async_copy(trace_hbm, trace_ref, lsem.at[4]),
        pltpu.make_async_copy(perm_hbm, perm_ref, lsem.at[5]),
        pltpu.make_async_copy(neigh_hbm, neigh_ref, lsem.at[6]),
        pltpu.make_async_copy(farl_hbm, farl_ref, lsem.at[7]),
        pltpu.make_async_copy(live_hbm, live_ref, lsem.at[8]),
    ]
    for load in smalls:
        load.start()

    barrier = pltpu.get_barrier_semaphore()
    side_peers = [y_peer(k) for k in range(1, YN)] + [e_peer(k) for k in range(1, 8)]
    for i in range(ZN - 1):
        at = line_at(i)

        @pl.when(second | ((at > z) & jnp.logical_not(origin & (at >= ZN // 2))))
        def _():
            signal(barrier, line_peer(at))

    @pl.when(direct)
    def _():
        for peer in side_peers:
            signal(barrier, peer)

    @pl.when(first & is_end)
    def _():
        signal(barrier, touching)

    loads = [
        pltpu.make_async_copy(stiff_hbm, stiff_v, lsem.at[0]),
        pltpu.make_async_copy(exc_hbm, exc_v, lsem.at[1]),
        pltpu.make_async_copy(basis_hbm, basis_v, lsem.at[2]),
        pltpu.make_async_copy(far_hbm, far_v, lsem.at[3]),
    ]
    for load in loads:
        load.start()
    for load in smalls:
        load.wait()

    own = jnp.concatenate([trace_ref[:, q * PATCH : (q + 1) * PATCH] for q in range(QN)], axis=0)
    high, low = split2(own)
    own_hi[...] = high
    own_lo[...] = low
    rows_hi[z] = high
    rows_lo[z] = low
    tab_v[0, 0:4, :] = perm_ref[0]
    for j in range(NB):
        tab_v[0, 4 + j : 5 + j, :] = jnp.full((1, PATCH), neigh_ref[0, j], jnp.int32)
    for f in range(FAR):
        tab_v[0, 8 + f : 9 + f, :] = jnp.full((1, PATCH), farl_ref[0, f], jnp.int32)
    tab_v[0, 10:16, :] = jnp.zeros((6, PATCH), jnp.int32)
    live = live_ref[0]
    centre, steps = cheb_constants()

    def remote(src, dst, send, recv, peer):
        return pltpu.make_async_remote_copy(
            src_ref=src,
            dst_ref=dst,
            send_sem=send,
            recv_sem=recv,
            device_id=peer,
            device_id_type=MESH,
        )

    def z_start(own_ref, rows_ref, part, chosen):
        for i in range(ZN - 1):
            at = line_at(i)

            @pl.when(chosen(at))
            def _():
                remote(
                    own_ref, rows_ref.at[z], zs.at[part, at], zr.at[part, z], line_peer(at)
                ).start()

    def z_wait(own_ref, rows_ref, part, chosen):
        for i in range(ZN - 1):
            at = line_at(i)

            @pl.when(chosen(at))
            def _():
                remote(
                    own_ref, rows_ref.at[at], zs.at[part, at], zr.at[part, at], line_peer(at)
                ).wait_recv()

    def z_sent(own_ref, rows_ref, part, chosen):
        for i in range(ZN - 1):
            at = line_at(i)

            @pl.when(chosen(at))
            def _():
                remote(
                    own_ref, rows_ref.at[z], zs.at[part, at], zr.at[part, z], line_peer(at)
                ).wait_send()

    t_copies = [
        remote(tab_v.at[0], tab_v.at[YN - k], ts.at[k], tr.at[k], y_peer(k)) for k in range(1, YN)
    ]

    def reaches(at):
        return jnp.logical_not(beyond & (at == 0))

    half_rows = rows_hi.at[ZN // 2 : ZN]
    passed = remote(half_rows, half_rows, hs.at[0], hr.at[0], (jnp.where(relay, 0, 1) * YN + y, sub))

    def meet_and_send():
        expected = jnp.where(second, ZN - 1, z - beyond.astype(jnp.int32)) + len(side_peers) * direct.astype(jnp.int32)
        pl.semaphore_wait(barrier, expected + (second & is_end).astype(jnp.int32))

        @pl.when(second & is_end)
        def _():
            for k in range(1, 8):
                signal(side_sem, e_peer(k))

        z_start(own_hi, rows_hi, 0, lambda at: second | ((at < z) & reaches(at)))
        for i in range(ZN - 1):
            at = line_at(i)

            @pl.when(first & (at < z) & reaches(at))
            def _():
                signal(up_sem, line_peer(at))

        @pl.when(direct)
        def _():
            for copy in t_copies:
                copy.start()

        @pl.when(second & is_end)
        def _():
            pl.semaphore_wait(side_sem, 7)
            signal(ready_sem, touching)

    def answer_line():
        @pl.when(z < ZN - 1)
        def _():
            pl.semaphore_wait(up_sem, jnp.where(origin, ZN // 2 - 1, ZN - 1 - z))

        @pl.when(relay)
        def _():
            z_wait(own_hi, rows_hi, 0, lambda at: at >= ZN // 2)
            passed.start()

        @pl.when(origin)
        def _():
            z_start(own_hi, rows_hi, 0, lambda at: (at > z) & (at < ZN // 2))
            passed.wait_recv()

        @pl.when(z == 0)
        def _():
            for k in range(1, 8):
                signal(side_sem, e_peer(k))

        @pl.when(hub)
        def _():
            for peer in side_peers:
                signal(side_sem, peer)

        z_start(own_hi, rows_hi, 0, lambda at: (at > z) & jnp.logical_not(origin & (at < ZN // 2)))

        @pl.when(hub)
        def _():
            pl.semaphore_wait(side_sem, len(side_peers))
            for at in range(ZN // 2, ZN):
                signal(hub_sem, line_peer(at))

    def pass_on():
        for k in range(1, 8):
            signal(ready_sem, line_peer(jnp.where(z == 0, k, ZN - 1 - k)))

    def return_word():
        pl.semaphore_wait(ready_sem, 1)
        signal(ready_sem, touching)
        pass_on()

    def local_work():
        smooth_part()
        prepare_part()

    def smooth_part():
        loads[0].wait()
        row = iota((BLK, BLK), 0)
        col = iota((BLK, BLK), 1)
        operator = stiff_v[0] + jnp.where((row == col) & (row < TROW), robin_gain, 0.0)
        a_high, a_low = split2(operator)
        a3[:, 0:BLK] = a_high
        a3[:, BLK : 2 * BLK] = a_low
        a3[:, 2 * BLK : 3 * BLK] = a_high

        loads[1].wait()
        column = sub * COLS + iota((BLK, COLS), 1)
        r_v[:, 0:COLS] = jnp.where(column < live, exc_v[0].astype(F32), 0.0)
        r_v[:, COLS:] = jnp.where(iota((BLK, PATCH), 0) == iota((BLK, PATCH), 1) % TROW, 1.0, 0.0)
        first = r_v[...] * (1.0 / centre)
        u_v[...] = first
        x_v[...] = first

        def smooth(step, carry):
            u_high, u_low = split2(u_v[...])
            moved = jnp.dot(
                a3[...],
                jnp.concatenate([u_high, u_high, u_low], axis=0),
                preferred_element_type=F32,
            )
            res = r_v[...] - moved
            r_v[...] = res
            keep, add = steps[0]
            for at in range(1, DEG - 1):
                keep = jnp.where(step == at, steps[at][0], keep)
                add = jnp.where(step == at, steps[at][1], add)
            following = keep * u_v[...] + add * res
            u_v[...] = following
            x_v[...] += following
            return carry

        lax.fori_loop(0, DEG - 1, smooth, 0)

    lane = iota((PATCH, PATCH), 1)
    sublane = iota((PATCH, PATCH), 0)

    def prepare_part():
        loads[2].wait()
        for r in range(OWN):
            basis_d[r] = basis_v[0, r : r + 1, :].astype(F32).reshape(256, PATCH)

        g_high, g_low = split2(x_v[:, COLS:])
        g3_v[:, 0:PATCH] = g_high
        g3_v[:, PATCH : 2 * PATCH] = g_high
        g3_v[:, 2 * PATCH :] = g_low
        tiled = jnp.concatenate([x_v[0:TROW, COLS:]] * QN, axis=0)
        gain = jnp.where(lane // TROW == sublane // TROW, (2.0 * robin_gain) * tiled, 0.0)
        b_high, b_low = split2(gain)
        b3_v[:, 0:PATCH] = b_high
        b3_v[:, PATCH : 2 * PATCH] = b_high
        b3_v[:, 2 * PATCH :] = b_low

        pieces = split3((2.0 * robin_gain) * x_v[0:TROW, 0:COLS])
        stacked = jnp.concatenate([piece.astype(F32) for piece in pieces], axis=0).astype(BF16)
        spread = iota((COLS, PATCH), 1) // TROW
        place = iota((COLS, PATCH), 0)
        keep = iota((TROW, PATCH), 0) == iota((TROW, PATCH), 1) % TROW
        for q in range(QN):
            pick = jnp.where(place == q * 16 + spread, 1.0, 0.0).astype(BF16)
            got = jnp.dot(stacked, pick, preferred_element_type=F32)
            got = got[0:8] + got[8:16] + got[16:24]
            t0_v[q : q + 1, :] = jnp.sum(jnp.where(keep, got, 0.0), axis=0, keepdims=True)

    def phase(at, carry):
        @pl.when((at == 0) == first)
        def _():
            meet_and_send()

        @pl.when(at == 0)
        def _():
            local_work()

        return carry

    lax.fori_loop(0, 2, phase, 0)

    @pl.when(first)
    def _():
        answer_line()

    @pl.when(jnp.logical_not(direct))
    def _():
        pl.semaphore_wait(hub_sem, 1)
        for copy in t_copies:
            copy.start()

    @pl.when(first & (z == ZN - 1))
    def _():
        return_word()

    @pl.when(second & is_end)
    def _():
        pl.semaphore_wait(ready_sem, 1)
        pass_on()

    for copy in t_copies:
        copy.wait_recv()
    for t in range(YN):
        for j in range(NB):
            hit = tab_v[t, j : j + 1, :] == sublane
            sel_v[t, j * PATCH : (j + 1) * PATCH, :] = jnp.where(hit, 1.0, 0.0).astype(BF16)

    loads[3].wait()
    z_wait(own_hi, rows_hi, 0, lambda at: jnp.logical_not((relay | origin) & (at >= ZN // 2)))

    def pick_row(t, entry, rows):
        wanted = jnp.broadcast_to(tab_v[t, entry : entry + 1, :], (QN, PATCH))
        found = jnp.zeros((QN, PATCH), F32)
        for k in range(ZN):
            found = jnp.where(wanted == k * YN + y, rows[k], found)
        return found

    f_copies = []
    high_rows = [rows_hi[k].astype(F32) for k in range(ZN)]
    for t in (2, 1, 3, 0):
        for f in range(FAR):
            fsend[t, f] = pick_row(t, 8 + f, high_rows).astype(BF16)
        if t:
            copy = remote(fsend.at[t], frecv.at[t], fs.at[t], fr.at[t], y_peer(t))
            copy.start()
            f_copies.append(copy)
    @pl.when(first & (z == 0))
    def _():
        pl.semaphore_wait(side_sem, 7)
        return_word()


    for copy in f_copies:
        copy.wait_recv()
    partial = jnp.zeros((8, RANK), F32)
    for f in range(FAR):
        remote_rows = fsend[0, f].astype(F32)
        for t in range(1, YN):
            remote_rows += frecv[t, f].astype(F32)
        flat = jnp.concatenate([remote_rows[q : q + 1, :] for q in range(QN)], axis=1)
        flat = jnp.broadcast_to(flat, (8, QN * PATCH)).astype(BF16)
        partial += dot_nt(flat, far_v[0, f])
    csend[:, 0:RANK] = partial[0:1, :]
    csend[:, RANK:] = jnp.zeros((1, 256 - RANK), F32)
    crecv[0] = csend[...]

    @pl.when(jnp.logical_not(is_end))
    def _():
        pl.semaphore_wait(ready_sem, 1)

    c_copies = []
    for dh in (1, 0):
        for dx in (2, 1, 3, 0):
            for dc in (0, 1):
                at = dh * 8 + dx * 2 + dc
                if at:
                    copy = remote(csend, crecv.at[at], cs.at[at], cr.at[at], s_peer(dx, dh, dc))
                    copy.start()
                    c_copies.append(copy)
    z_start(own_lo, rows_lo, 1, lambda at: at >= 0)
    for copy in c_copies:
        copy.wait_recv()

    total = crecv[0]
    for k in range(1, SUB):
        total += crecv[k]
    total = total.astype(BF16).astype(F32)
    mine = iota((16, 256), 1) == sub * OWN + iota((16, 256), 0)
    shares = jnp.sum(jnp.where(mine, jnp.broadcast_to(total, (16, 256)), 0.0), axis=1, keepdims=True)
    weights = [jnp.broadcast_to(shares[r : r + 1, :], (QN, PATCH)) for r in range(OWN)]
    for xx in range(XN):
        for hh in range(2):
            for cc in range(2):
                at = (xx * 4 + hh * 2 + cc) * QN
                value = weights[0] * basis_d[0, at : at + QN, :]
                for r in range(1, OWN):
                    value += weights[r] * basis_d[r, at : at + QN, :]
                psend[hh, xx * 2 + cc] = value
    psend_b[...] = psend[1 - h].astype(BF16)
    p_copies = [[], []]
    for k in (4, 5, 3, 2, 6, 1, 7, 0):
        at = (s8 + k) % 8
        peer = (dom, (at // 2) * 4 + (1 - h) * 2 + at % 2)
        copy = remote(psend_b.at[at], precv_b.at[k], ps.at[0, k], pr.at[0, k], peer)
        copy.start()
        p_copies[0].append(copy)
    for k in range(1, 8):
        copy = remote(psend.at[h, (s8 + k) % 8], precv.at[k], ps.at[1, k], pr.at[1, k], e_peer(k))
        copy.start()
        p_copies[1].append(copy)

    z_wait(own_lo, rows_lo, 1, lambda at: at >= 0)
    full_rows = [rows_hi[k].astype(F32) + rows_lo[k].astype(F32) for k in range(ZN)]
    n_copies = []
    for t in (2, 1, 3, 0):
        faces = jnp.concatenate([pick_row(t, 4 + j, full_rows) for j in range(NB)], axis=1)
        got = jnp.dot(
            jnp.concatenate(split2(faces), axis=0), sel_v[t], preferred_element_type=F32
        )
        nsend[t] = got[0:QN] + got[QN:]
        if t:
            copy = remote(nsend.at[t], nrecv.at[t], ns.at[t], nr.at[t], y_peer(t))
            copy.start()
            n_copies.append(copy)

    for copy in n_copies:
        copy.wait_recv()
    near = (nsend[0] + nrecv[1]) + (nrecv[2] + nrecv[3])
    for copy in p_copies[1]:
        copy.wait_recv()
    far = psend[h, s8]
    for k in range(1, 8):
        far += precv[k]
    for copy in p_copies[0]:
        copy.wait_recv()
    for k in range(8):
        far += precv_b[k].astype(F32)
    incoming = near + far

    patch_col = sub * COLS + iota((QN, PATCH), 0) * 16 + iota((QN, PATCH), 1) // TROW
    live_trace = patch_col < live
    incoming = jnp.where(live_trace, incoming, 0.0)
    i_high, i_low = split2(incoming)
    i3 = jnp.concatenate([i_high, i_low, i_high], axis=1)
    outgoing = t0_v[...] + dot_nt(i3, b3_v[...]) - incoming
    outgoing = jnp.where(live_trace, outgoing, 0.0)
    for q in range(QN):
        next_ref[:, q * PATCH : (q + 1) * PATCH] = outgoing[q : q + 1, :]

    lanes3 = (iota((16, 3 * PATCH), 1) % PATCH) // TROW == iota((16, 3 * PATCH), 0)
    i3f = i3.astype(F32)
    wide = jnp.concatenate(
        [
            jnp.where(lanes3, jnp.broadcast_to(i3f[q : q + 1, :], (16, 3 * PATCH)), 0.0)
            for q in range(QN)
        ],
        axis=0,
    ).astype(BF16)
    field_ref[0] = x_v[:, 0:COLS] + dot_nt(g3_v[...], wide)

    z_sent(own_hi, rows_hi, 0, reaches)

    @pl.when(relay)
    def _():
        passed.wait_send()

    z_sent(own_lo, rows_lo, 1, lambda at: at >= 0)
    for copy in t_copies + f_copies + n_copies + c_copies + p_copies[0] + p_copies[1]:
        copy.wait_send()


def body(*operands):
    vmem = pl.BlockSpec(memory_space=pltpu.VMEM)
    hbm = pl.BlockSpec(memory_space=pltpu.HBM)
    dma = pltpu.SemaphoreType.DMA
    patches = (QN, PATCH)
    return pl.pallas_call(
        kernel,
        out_shape=(
            jax.ShapeDtypeStruct((1, BLK, COLS), F32),
            jax.ShapeDtypeStruct((1, QN * PATCH), F32),
        ),
        in_specs=[hbm] * 9,
        out_specs=(vmem, vmem),
        scratch_shapes=[
            pltpu.VMEM((1, QN * PATCH), F32),
            pltpu.SMEM((1, NB), jnp.int32),
            pltpu.SMEM((1, FAR), jnp.int32),
            pltpu.VMEM((1, NB, PATCH), jnp.int32),
            pltpu.SMEM((1,), jnp.int32),
            pltpu.VMEM((1, BLK, COLS), BF16),
            pltpu.VMEM((1, BLK, BLK), F32),
            pltpu.VMEM((1, FAR, RANK, QN * PATCH), BF16),
            pltpu.VMEM((1, OWN, SUB * QN * PATCH), BF16),
            pltpu.VMEM((OWN, SUB * QN, PATCH), F32),
            pltpu.VMEM((BLK, 3 * BLK), BF16),
            pltpu.VMEM((BLK, VCOLS), F32),
            pltpu.VMEM((BLK, VCOLS), F32),
            pltpu.VMEM((BLK, VCOLS), F32),
            pltpu.VMEM(patches, BF16),
            pltpu.VMEM(patches, BF16),
            pltpu.VMEM((ZN,) + patches, BF16),
            pltpu.VMEM((ZN,) + patches, BF16),
            pltpu.VMEM((YN, 16, PATCH), jnp.int32),
            pltpu.VMEM((YN, NB * PATCH, PATCH), BF16),
            pltpu.VMEM((YN, FAR) + patches, BF16),
            pltpu.VMEM((YN, FAR) + patches, BF16),
            pltpu.VMEM((YN,) + patches, F32),
            pltpu.VMEM((YN,) + patches, F32),
            pltpu.VMEM((1, 256), F32),
            pltpu.VMEM((SUB, 1, 256), F32),
            pltpu.VMEM((2, 8) + patches, F32),
            pltpu.VMEM((8,) + patches, F32),
            pltpu.VMEM((8,) + patches, BF16),
            pltpu.VMEM((8,) + patches, BF16),
            pltpu.VMEM(patches, F32),
            pltpu.VMEM((BLK, 3 * PATCH), BF16),
            pltpu.VMEM((PATCH, 3 * PATCH), BF16),
            dma((9,)),
            dma((2, ZN)),
            dma((2, ZN)),
            dma((YN,)),
            dma((YN,)),
            dma((YN,)),
            dma((YN,)),
            dma((YN,)),
            dma((YN,)),
            dma((SUB,)),
            dma((SUB,)),
            dma((2, 8)),
            dma((2, 8)),
            dma((1,)),
            dma((1,)),
            pltpu.SemaphoreType.REGULAR,
            pltpu.SemaphoreType.REGULAR,
            pltpu.SemaphoreType.REGULAR,
            pltpu.SemaphoreType.REGULAR,
        ],
        name="robin_sweep",
        compiler_params=pltpu.CompilerParams(
            collective_id=0, has_side_effects=True, vmem_limit_bytes=40 * 1024 * 1024
        ),
    )(*[o if o.ndim == 1 else pltpu.with_memory_space_constraint(o, pltpu.HBM) for o in operands])


def solution(mesh):
    placed = (
        P("dom", None, "sub"),
        P("dom", None, None),
        P("dom", "sub"),
        P("dom", None),
        P("dom", None),
        P("dom", None, None),
        P("dom"),
        P("dom", None, None, "sub"),
        P("dom", "sub", None),
    )
    return jax.shard_map(
        body,
        mesh=mesh,
        in_specs=placed,
        out_specs=(P("dom", None, "sub"), P("dom", "sub")),
        check_vma=False,
    )
```

```python
import functools
import jax
import jax.numpy as jnp
from jax import lax
from jax.experimental import pallas as pl
from jax.experimental.pallas import tpu as pltpu
from jax.sharding import PartitionSpec as P

MESH = pl.DeviceIdType.MESH
F32 = jnp.float32
BF16 = jnp.bfloat16

BLK = 512
TROW = 8
NB = 4
FAR = 2
DEG = 8
PATCH = 128
RANK = 192
ZN, YN, XN = 16, 4, 4
SUB = 16
OWN = RANK // SUB
QN = 16
COLS = 256
VCOLS = COLS + PATCH

cheb_lower = 0.8
cheb_upper = 24.0
robin_gain = 2.0


def cheb_constants():
    centre = 0.5 * (cheb_upper + cheb_lower)
    half = 0.5 * (cheb_upper - cheb_lower)
    ratio = centre / half
    previous = 1.0 / ratio
    steps = []
    for _ in range(DEG - 1):
        following = 1.0 / (2.0 * ratio - previous)
        steps.append((following * previous, 2.0 * following / half))
        previous = following
    return centre, steps


def split2(values):
    high = values.astype(BF16)
    low = (values - high.astype(F32)).astype(BF16)
    return high, low


def split3(values):
    high = values.astype(BF16)
    rest = values - high.astype(F32)
    middle = rest.astype(BF16)
    low = (rest - middle.astype(F32)).astype(BF16)
    return high, middle, low


def dot_nt(left, right):
    return lax.dot_general(left, right, (((1,), (1,)), ((), ())), preferred_element_type=F32)


def iota(shape, axis):
    return lax.broadcasted_iota(jnp.int32, shape, axis)


def kernel(
    exc_hbm,
    stiff_hbm,
    trace_hbm,
    neigh_hbm,
    farl_hbm,
    perm_hbm,
    live_hbm,
    far_hbm,
    basis_hbm,
    field_ref,
    next_ref,
    trace_ref,
    neigh_ref,
    farl_ref,
    perm_ref,
    live_ref,
    exc_v,
    stiff_v,
    far_v,
    basis_v,
    basis_d,
    a3,
    u_v,
    r_v,
    x_v,
    own_hi,
    own_lo,
    rows_hi,
    rows_lo,
    tab_v,
    sel_v,
    fsend,
    frecv,
    nsend,
    nrecv,
    csend,
    crecv,
    psend,
    precv,
    psend_b,
    precv_b,
    t0_v,
    g3_v,
    b3_v,
    lsem,
    zs,
    zr,
    ts,
    tr,
    fs,
    fr,
    ns,
    nr,
    cs,
    cr,
    ps,
    pr,
    hs,
    hr,
    side_sem,
    ready_sem,
    hub_sem,
    up_sem,
):
    dom = lax.axis_index("dom")
    sub = lax.axis_index("sub")
    z, y = dom // YN, dom % YN
    x, h, c = sub // 4, (sub // 2) % 2, sub % 2
    s8 = x * 2 + c

    def z_peer(k):
        return (((z + k) % ZN) * YN + y, sub)

    def line_peer(at):
        return (at * YN + y, sub)

    def y_peer(k):
        return (z * YN + (y + k) % YN, sub)

    def s_peer(dx, dh, dc):
        return (dom, ((x + dx) % XN) * 4 + ((h + dh) % 2) * 2 + (c + dc) % 2)

    def e_peer(k):
        t = (s8 + k) % 8
        return (dom, (t // 2) * 4 + h * 2 + t % 2)

    first, second = h == 0, h == 1
    is_end = (z == 0) | (z == ZN - 1)
    touching = ((ZN - 1 - z) * YN + y, x * 4 + (1 - h) * 2 + c)
    direct = second | (z < ZN // 2)
    hub = first & (z == ZN // 2 - 1)

    special = first & (y == 0) & (x == 0) & (c == 0)
    beyond = special & (z >= ZN // 2)
    origin = special & (z == 0)
    relay = special & (z == 1)

    turned = jnp.where(z < ZN // 2, ZN - 1 - z, z)

    def line_at(i):
        place = i + (i >= turned).astype(jnp.int32)
        return jnp.where(z < ZN // 2, ZN - 1 - place, place)

    def signal(sem, peer):
        pl.semaphore_signal(sem, inc=1, device_id=peer, device_id_type=MESH)

    barrier = pltpu.get_barrier_semaphore()
    side_peers = [y_peer(k) for k in range(1, YN)] + [e_peer(k) for k in range(1, 8)]
    for i in range(ZN - 1):
        at = line_at(i)

        @pl.when(second | ((at > z) & jnp.logical_not(origin & (at >= ZN // 2))))
        def _():
            signal(barrier, line_peer(at))

    smalls = [
        pltpu.make_async_copy(trace_hbm, trace_ref, lsem.at[4]),
        pltpu.make_async_copy(perm_hbm, perm_ref, lsem.at[5]),
        pltpu.make_async_copy(neigh_hbm, neigh_ref, lsem.at[6]),
        pltpu.make_async_copy(farl_hbm, farl_ref, lsem.at[7]),
        pltpu.make_async_copy(live_hbm, live_ref, lsem.at[8]),
    ]
    for load in smalls:
        load.start()

    @pl.when(direct)
    def _():
        for peer in side_peers:
            signal(barrier, peer)

    @pl.when(first & is_end)
    def _():
        signal(barrier, touching)

    loads = [
        pltpu.make_async_copy(stiff_hbm, stiff_v, lsem.at[0]),
        pltpu.make_async_copy(exc_hbm, exc_v, lsem.at[1]),
        pltpu.make_async_copy(basis_hbm, basis_v, lsem.at[2]),
        pltpu.make_async_copy(far_hbm, far_v, lsem.at[3]),
    ]
    for load in loads:
        load.start()
    for load in smalls:
        load.wait()

    own = jnp.concatenate([trace_ref[:, q * PATCH : (q + 1) * PATCH] for q in range(QN)], axis=0)
    high, low = split2(own)
    own_hi[...] = high
    own_lo[...] = low
    rows_hi[z] = high
    rows_lo[z] = low
    tab_v[0, 0:4, :] = perm_ref[0]
    for j in range(NB):
        tab_v[0, 4 + j : 5 + j, :] = jnp.full((1, PATCH), neigh_ref[0, j], jnp.int32)
    for f in range(FAR):
        tab_v[0, 8 + f : 9 + f, :] = jnp.full((1, PATCH), farl_ref[0, f], jnp.int32)
    tab_v[0, 10:16, :] = jnp.zeros((6, PATCH), jnp.int32)
    live = live_ref[0]
    centre, steps = cheb_constants()

    def remote(src, dst, send, recv, peer):
        return pltpu.make_async_remote_copy(
            src_ref=src,
            dst_ref=dst,
            send_sem=send,
            recv_sem=recv,
            device_id=peer,
            device_id_type=MESH,
        )

    def z_start(own_ref, rows_ref, part, chosen):
        for i in range(ZN - 1):
            at = line_at(i)

            @pl.when(chosen(at))
            def _():
                remote(
                    own_ref, rows_ref.at[z], zs.at[part, at], zr.at[part, z], line_peer(at)
                ).start()

    def z_wait(own_ref, rows_ref, part, chosen):
        for i in range(ZN - 1):
            at = line_at(i)

            @pl.when(chosen(at))
            def _():
                remote(
                    own_ref, rows_ref.at[at], zs.at[part, at], zr.at[part, at], line_peer(at)
                ).wait_recv()

    def z_sent(own_ref, rows_ref, part, chosen):
        for i in range(ZN - 1):
            at = line_at(i)

            @pl.when(chosen(at))
            def _():
                remote(
                    own_ref, rows_ref.at[z], zs.at[part, at], zr.at[part, z], line_peer(at)
                ).wait_send()

    t_copies = [
        remote(tab_v.at[0], tab_v.at[YN - k], ts.at[k], tr.at[k], y_peer(k)) for k in range(1, YN)
    ]

    def reaches(at):
        return jnp.logical_not(beyond & (at == 0))

    half_rows = rows_hi.at[ZN // 2 : ZN]
    passed = remote(half_rows, half_rows, hs.at[0], hr.at[0], (jnp.where(relay, 0, 1) * YN + y, sub))

    def meet_and_send():
        expected = jnp.where(second, ZN - 1, z - beyond.astype(jnp.int32)) + len(side_peers) * direct.astype(jnp.int32)
        pl.semaphore_wait(barrier, expected + (second & is_end).astype(jnp.int32))

        @pl.when(second & is_end)
        def _():
            for k in range(1, 8):
                signal(side_sem, e_peer(k))

        z_start(own_hi, rows_hi, 0, lambda at: second | ((at < z) & reaches(at)))
        for i in range(ZN - 1):
            at = line_at(i)

            @pl.when(first & (at < z) & reaches(at))
            def _():
                signal(up_sem, line_peer(at))

        @pl.when(direct)
        def _():
            for copy in t_copies:
                copy.start()

        @pl.when(second & is_end)
        def _():
            pl.semaphore_wait(side_sem, 7)
            signal(ready_sem, touching)

    def answer_line():
        @pl.when(z < ZN - 1)
        def _():
            pl.semaphore_wait(up_sem, jnp.where(origin, ZN // 2 - 1, ZN - 1 - z))

        @pl.when(relay)
        def _():
            z_wait(own_hi, rows_hi, 0, lambda at: at >= ZN // 2)
            passed.start()

        @pl.when(origin)
        def _():
            z_start(own_hi, rows_hi, 0, lambda at: (at > z) & (at < ZN // 2))
            passed.wait_recv()

        @pl.when(z == 0)
        def _():
            for k in range(1, 8):
                signal(side_sem, e_peer(k))

        @pl.when(hub)
        def _():
            for peer in side_peers:
                signal(side_sem, peer)

        z_start(own_hi, rows_hi, 0, lambda at: (at > z) & jnp.logical_not(origin & (at < ZN // 2)))

        @pl.when(hub)
        def _():
            pl.semaphore_wait(side_sem, len(side_peers))
            for at in range(ZN // 2, ZN):
                signal(hub_sem, line_peer(at))

    def pass_on():
        for k in range(1, 8):
            signal(ready_sem, line_peer(jnp.where(z == 0, k, ZN - 1 - k)))

    def return_word():
        pl.semaphore_wait(ready_sem, 1)
        signal(ready_sem, touching)
        pass_on()

    def local_work():
        smooth_part()
        prepare_part()

    def smooth_part():
        loads[0].wait()
        row = iota((BLK, BLK), 0)
        col = iota((BLK, BLK), 1)
        operator = stiff_v[0] + jnp.where((row == col) & (row < TROW), robin_gain, 0.0)
        a_high, a_low = split2(operator)
        a3[:, 0:BLK] = a_high
        a3[:, BLK : 2 * BLK] = a_low
        a3[:, 2 * BLK : 3 * BLK] = a_high

        loads[1].wait()
        column = sub * COLS + iota((BLK, COLS), 1)
        r_v[:, 0:COLS] = jnp.where(column < live, exc_v[0].astype(F32), 0.0)
        r_v[:, COLS:] = jnp.where(iota((BLK, PATCH), 0) == iota((BLK, PATCH), 1) % TROW, 1.0, 0.0)
        first = r_v[...] * (1.0 / centre)
        u_v[...] = first
        x_v[...] = first

        def smooth(step, carry):
            u_high, u_low = split2(u_v[...])
            moved = jnp.dot(
                a3[...],
                jnp.concatenate([u_high, u_high, u_low], axis=0),
                preferred_element_type=F32,
            )
            res = r_v[...] - moved
            r_v[...] = res
            keep, add = steps[0]
            for at in range(1, DEG - 1):
                keep = jnp.where(step == at, steps[at][0], keep)
                add = jnp.where(step == at, steps[at][1], add)
            following = keep * u_v[...] + add * res
            u_v[...] = following
            x_v[...] += following
            return carry

        lax.fori_loop(0, DEG - 1, smooth, 0)

    lane = iota((PATCH, PATCH), 1)
    sublane = iota((PATCH, PATCH), 0)

    def prepare_part():
        loads[2].wait()
        for r in range(OWN):
            basis_d[r] = basis_v[0, r : r + 1, :].astype(F32).reshape(256, PATCH)

        g_high, g_low = split2(x_v[:, COLS:])
        g3_v[:, 0:PATCH] = g_high
        g3_v[:, PATCH : 2 * PATCH] = g_high
        g3_v[:, 2 * PATCH :] = g_low
        tiled = jnp.concatenate([x_v[0:TROW, COLS:]] * QN, axis=0)
        gain = jnp.where(lane // TROW == sublane // TROW, (2.0 * robin_gain) * tiled, 0.0)
        b_high, b_low = split2(gain)
        b3_v[:, 0:PATCH] = b_high
        b3_v[:, PATCH : 2 * PATCH] = b_high
        b3_v[:, 2 * PATCH :] = b_low

        pieces = split3((2.0 * robin_gain) * x_v[0:TROW, 0:COLS])
        stacked = jnp.concatenate([piece.astype(F32) for piece in pieces], axis=0).astype(BF16)
        spread = iota((COLS, PATCH), 1) // TROW
        place = iota((COLS, PATCH), 0)
        keep = iota((TROW, PATCH), 0) == iota((TROW, PATCH), 1) % TROW
        for q in range(QN):
            pick = jnp.where(place == q * 16 + spread, 1.0, 0.0).astype(BF16)
            got = jnp.dot(stacked, pick, preferred_element_type=F32)
            got = got[0:8] + got[8:16] + got[16:24]
            t0_v[q : q + 1, :] = jnp.sum(jnp.where(keep, got, 0.0), axis=0, keepdims=True)

    def phase(at, carry):
        @pl.when((at == 0) == first)
        def _():
            meet_and_send()

        @pl.when(at == 0)
        def _():
            local_work()

        return carry

    lax.fori_loop(0, 2, phase, 0)

    @pl.when(first)
    def _():
        answer_line()

    @pl.when(jnp.logical_not(direct))
    def _():
        pl.semaphore_wait(hub_sem, 1)
        for copy in t_copies:
            copy.start()

    @pl.when(first & (z == ZN - 1))
    def _():
        return_word()

    @pl.when(second & is_end)
    def _():
        pl.semaphore_wait(ready_sem, 1)
        pass_on()

    for copy in t_copies:
        copy.wait_recv()
    for t in range(YN):
        for j in range(NB):
            hit = tab_v[t, j : j + 1, :] == sublane
            sel_v[t, j * PATCH : (j + 1) * PATCH, :] = jnp.where(hit, 1.0, 0.0).astype(BF16)

    loads[3].wait()
    z_wait(own_hi, rows_hi, 0, lambda at: jnp.logical_not((relay | origin) & (at >= ZN // 2)))

    def pick_row(t, entry, rows):
        wanted = jnp.broadcast_to(tab_v[t, entry : entry + 1, :], (QN, PATCH))
        found = jnp.zeros((QN, PATCH), F32)
        for k in range(ZN):
            found = jnp.where(wanted == k * YN + y, rows[k], found)
        return found

    f_copies = []
    high_rows = [rows_hi[k].astype(F32) for k in range(ZN)]
    for t in (2, 1, 3, 0):
        for f in range(FAR):
            fsend[t, f] = pick_row(t, 8 + f, high_rows).astype(BF16)
        if t:
            copy = remote(fsend.at[t], frecv.at[t], fs.at[t], fr.at[t], y_peer(t))
            copy.start()
            f_copies.append(copy)
    @pl.when(first & (z == 0))
    def _():
        pl.semaphore_wait(side_sem, 7)
        return_word()


    for copy in f_copies:
        copy.wait_recv()
    partial = jnp.zeros((8, RANK), F32)
    for f in range(FAR):
        remote_rows = fsend[0, f].astype(F32)
        for t in range(1, YN):
            remote_rows += frecv[t, f].astype(F32)
        flat = jnp.concatenate([remote_rows[q : q + 1, :] for q in range(QN)], axis=1)
        flat = jnp.broadcast_to(flat, (8, QN * PATCH)).astype(BF16)
        partial += dot_nt(flat, far_v[0, f])
    csend[:, 0:RANK] = partial[0:1, :]
    csend[:, RANK:] = jnp.zeros((1, 256 - RANK), F32)
    crecv[0] = csend[...]

    @pl.when(jnp.logical_not(is_end))
    def _():
        pl.semaphore_wait(ready_sem, 1)

    c_copies = []
    for dh in (1, 0):
        for dx in (2, 1, 3, 0):
            for dc in (0, 1):
                at = dh * 8 + dx * 2 + dc
                if at:
                    copy = remote(csend, crecv.at[at], cs.at[at], cr.at[at], s_peer(dx, dh, dc))
                    copy.start()
                    c_copies.append(copy)
    z_start(own_lo, rows_lo, 1, lambda at: at >= 0)
    for copy in c_copies:
        copy.wait_recv()

    total = crecv[0]
    for k in range(1, SUB):
        total += crecv[k]
    total = total.astype(BF16).astype(F32)
    mine = iota((16, 256), 1) == sub * OWN + iota((16, 256), 0)
    shares = jnp.sum(jnp.where(mine, jnp.broadcast_to(total, (16, 256)), 0.0), axis=1, keepdims=True)
    weights = [jnp.broadcast_to(shares[r : r + 1, :], (QN, PATCH)) for r in range(OWN)]
    for xx in range(XN):
        for hh in range(2):
            for cc in range(2):
                at = (xx * 4 + hh * 2 + cc) * QN
                value = weights[0] * basis_d[0, at : at + QN, :]
                for r in range(1, OWN):
                    value += weights[r] * basis_d[r, at : at + QN, :]
                psend[hh, xx * 2 + cc] = value
    psend_b[...] = psend[1 - h].astype(BF16)
    p_copies = [[], []]
    for k in (4, 5, 3, 2, 6, 1, 7, 0):
        at = (s8 + k) % 8
        peer = (dom, (at // 2) * 4 + (1 - h) * 2 + at % 2)
        copy = remote(psend_b.at[at], precv_b.at[k], ps.at[0, k], pr.at[0, k], peer)
        copy.start()
        p_copies[0].append(copy)
    for k in range(1, 8):
        copy = remote(psend.at[h, (s8 + k) % 8], precv.at[k], ps.at[1, k], pr.at[1, k], e_peer(k))
        copy.start()
        p_copies[1].append(copy)

    z_wait(own_lo, rows_lo, 1, lambda at: at >= 0)
    full_rows = [rows_hi[k].astype(F32) + rows_lo[k].astype(F32) for k in range(ZN)]
    n_copies = []
    for t in (2, 1, 3, 0):
        faces = jnp.concatenate([pick_row(t, 4 + j, full_rows) for j in range(NB)], axis=1)
        got = jnp.dot(
            jnp.concatenate(split2(faces), axis=0), sel_v[t], preferred_element_type=F32
        )
        nsend[t] = got[0:QN] + got[QN:]
        if t:
            copy = remote(nsend.at[t], nrecv.at[t], ns.at[t], nr.at[t], y_peer(t))
            copy.start()
            n_copies.append(copy)

    z_sent(own_hi, rows_hi, 0, reaches)

    @pl.when(relay)
    def _():
        passed.wait_send()

    z_sent(own_lo, rows_lo, 1, lambda at: at >= 0)
    for copy in t_copies + f_copies + c_copies + p_copies[1]:
        copy.wait_send()
    for copy in n_copies:
        copy.wait_recv()
    for copy in n_copies:
        copy.wait_send()
    near = (nsend[0] + nrecv[1]) + (nrecv[2] + nrecv[3])
    for copy in p_copies[1]:
        copy.wait_recv()
    far = psend[h, s8]
    for k in range(1, 8):
        far += precv[k]
    for copy in p_copies[0]:
        copy.wait_recv()
    for k in range(8):
        far += precv_b[k].astype(F32)
    incoming = near + far

    patch_col = sub * COLS + iota((QN, PATCH), 0) * 16 + iota((QN, PATCH), 1) // TROW
    live_trace = patch_col < live
    incoming = jnp.where(live_trace, incoming, 0.0)
    i_high, i_low = split2(incoming)
    i3 = jnp.concatenate([i_high, i_low, i_high], axis=1)
    outgoing = t0_v[...] + dot_nt(i3, b3_v[...]) - incoming
    outgoing = jnp.where(live_trace, outgoing, 0.0)
    for q in range(QN):
        next_ref[:, q * PATCH : (q + 1) * PATCH] = outgoing[q : q + 1, :]

    lanes3 = (iota((16, 3 * PATCH), 1) % PATCH) // TROW == iota((16, 3 * PATCH), 0)
    i3f = i3.astype(F32)
    wide = jnp.concatenate(
        [
            jnp.where(lanes3, jnp.broadcast_to(i3f[q : q + 1, :], (16, 3 * PATCH)), 0.0)
            for q in range(QN)
        ],
        axis=0,
    ).astype(BF16)
    field_ref[0] = x_v[:, 0:COLS] + dot_nt(g3_v[...], wide)

    for copy in p_copies[0]:
        copy.wait_send()


def body(*operands):
    vmem = pl.BlockSpec(memory_space=pltpu.VMEM)
    hbm = pl.BlockSpec(memory_space=pltpu.HBM)
    dma = pltpu.SemaphoreType.DMA
    patches = (QN, PATCH)
    return pl.pallas_call(
        kernel,
        out_shape=(
            jax.ShapeDtypeStruct((1, BLK, COLS), F32),
            jax.ShapeDtypeStruct((1, QN * PATCH), F32),
        ),
        in_specs=[hbm] * 9,
        out_specs=(vmem, vmem),
        scratch_shapes=[
            pltpu.VMEM((1, QN * PATCH), F32),
            pltpu.SMEM((1, NB), jnp.int32),
            pltpu.SMEM((1, FAR), jnp.int32),
            pltpu.VMEM((1, NB, PATCH), jnp.int32),
            pltpu.SMEM((1,), jnp.int32),
            pltpu.VMEM((1, BLK, COLS), BF16),
            pltpu.VMEM((1, BLK, BLK), F32),
            pltpu.VMEM((1, FAR, RANK, QN * PATCH), BF16),
            pltpu.VMEM((1, OWN, SUB * QN * PATCH), BF16),
            pltpu.VMEM((OWN, SUB * QN, PATCH), F32),
            pltpu.VMEM((BLK, 3 * BLK), BF16),
            pltpu.VMEM((BLK, VCOLS), F32),
            pltpu.VMEM((BLK, VCOLS), F32),
            pltpu.VMEM((BLK, VCOLS), F32),
            pltpu.VMEM(patches, BF16),
            pltpu.VMEM(patches, BF16),
            pltpu.VMEM((ZN,) + patches, BF16),
            pltpu.VMEM((ZN,) + patches, BF16),
            pltpu.VMEM((YN, 16, PATCH), jnp.int32),
            pltpu.VMEM((YN, NB * PATCH, PATCH), BF16),
            pltpu.VMEM((YN, FAR) + patches, BF16),
            pltpu.VMEM((YN, FAR) + patches, BF16),
            pltpu.VMEM((YN,) + patches, F32),
            pltpu.VMEM((YN,) + patches, F32),
            pltpu.VMEM((1, 256), F32),
            pltpu.VMEM((SUB, 1, 256), F32),
            pltpu.VMEM((2, 8) + patches, F32),
            pltpu.VMEM((8,) + patches, F32),
            pltpu.VMEM((8,) + patches, BF16),
            pltpu.VMEM((8,) + patches, BF16),
            pltpu.VMEM(patches, F32),
            pltpu.VMEM((BLK, 3 * PATCH), BF16),
            pltpu.VMEM((PATCH, 3 * PATCH), BF16),
            dma((9,)),
            dma((2, ZN)),
            dma((2, ZN)),
            dma((YN,)),
            dma((YN,)),
            dma((YN,)),
            dma((YN,)),
            dma((YN,)),
            dma((YN,)),
            dma((SUB,)),
            dma((SUB,)),
            dma((2, 8)),
            dma((2, 8)),
            dma((1,)),
            dma((1,)),
            pltpu.SemaphoreType.REGULAR,
            pltpu.SemaphoreType.REGULAR,
            pltpu.SemaphoreType.REGULAR,
            pltpu.SemaphoreType.REGULAR,
        ],
        name="robin_sweep",
        compiler_params=pltpu.CompilerParams(
            collective_id=0, has_side_effects=True, vmem_limit_bytes=40 * 1024 * 1024
        ),
    )(*[o if o.ndim == 1 else pltpu.with_memory_space_constraint(o, pltpu.HBM) for o in operands])


def solution(mesh):
    placed = (
        P("dom", None, "sub"),
        P("dom", None, None),
        P("dom", "sub"),
        P("dom", None),
        P("dom", None),
        P("dom", None, None),
        P("dom"),
        P("dom", None, None, "sub"),
        P("dom", "sub", None),
    )
    return jax.shard_map(
        body,
        mesh=mesh,
        in_specs=placed,
        out_specs=(P("dom", None, "sub"), P("dom", "sub")),
        check_vma=False,
    )
```

```python
import functools
import jax
import jax.numpy as jnp
from jax import lax
from jax.experimental import pallas as pl
from jax.experimental.pallas import tpu as pltpu
from jax.sharding import PartitionSpec as P

MESH = pl.DeviceIdType.MESH
F32 = jnp.float32
BF16 = jnp.bfloat16

BLK = 512
TROW = 8
NB = 4
FAR = 2
DEG = 8
PATCH = 128
RANK = 192
ZN, YN, XN = 16, 4, 4
SUB = 16
OWN = RANK // SUB
QN = 16
COLS = 256
VCOLS = COLS + PATCH

cheb_lower = 0.8
cheb_upper = 24.0
robin_gain = 2.0


def cheb_constants():
    centre = 0.5 * (cheb_upper + cheb_lower)
    half = 0.5 * (cheb_upper - cheb_lower)
    ratio = centre / half
    previous = 1.0 / ratio
    steps = []
    for _ in range(DEG - 1):
        following = 1.0 / (2.0 * ratio - previous)
        steps.append((following * previous, 2.0 * following / half))
        previous = following
    return centre, steps


def split2(values):
    high = values.astype(BF16)
    low = (values - high.astype(F32)).astype(BF16)
    return high, low


def split3(values):
    high = values.astype(BF16)
    rest = values - high.astype(F32)
    middle = rest.astype(BF16)
    low = (rest - middle.astype(F32)).astype(BF16)
    return high, middle, low


def dot_nt(left, right):
    return lax.dot_general(left, right, (((1,), (1,)), ((), ())), preferred_element_type=F32)


def iota(shape, axis):
    return lax.broadcasted_iota(jnp.int32, shape, axis)


def kernel(
    exc_hbm,
    stiff_hbm,
    trace_hbm,
    neigh_hbm,
    farl_hbm,
    perm_hbm,
    live_hbm,
    far_hbm,
    basis_hbm,
    field_ref,
    next_ref,
    trace_ref,
    neigh_ref,
    farl_ref,
    perm_ref,
    live_ref,
    exc_v,
    stiff_v,
    far_v,
    basis_v,
    basis_d,
    a3,
    u_v,
    r_v,
    x_v,
    own_hi,
    own_lo,
    rows_hi,
    rows_lo,
    tab_v,
    sel_v,
    fsend,
    frecv,
    nsend,
    nrecv,
    csend,
    crecv,
    psend,
    precv,
    psend_b,
    precv_b,
    t0_v,
    g3_v,
    b3_v,
    lsem,
    zs,
    zr,
    ts,
    tr,
    fs,
    fr,
    ns,
    nr,
    cs,
    cr,
    ps,
    pr,
    hs,
    hr,
    side_sem,
    ready_sem,
    hub_sem,
    up_sem,
):
    dom = lax.axis_index("dom")
    sub = lax.axis_index("sub")
    z, y = dom // YN, dom % YN
    x, h, c = sub // 4, (sub // 2) % 2, sub % 2
    s8 = x * 2 + c

    def z_peer(k):
        return (((z + k) % ZN) * YN + y, sub)

    def line_peer(at):
        return (at * YN + y, sub)

    def y_peer(k):
        return (z * YN + (y + k) % YN, sub)

    def s_peer(dx, dh, dc):
        return (dom, ((x + dx) % XN) * 4 + ((h + dh) % 2) * 2 + (c + dc) % 2)

    def e_peer(k):
        t = (s8 + k) % 8
        return (dom, (t // 2) * 4 + h * 2 + t % 2)

    first, second = h == 0, h == 1
    is_end = (z == 0) | (z == ZN - 1)
    touching = ((ZN - 1 - z) * YN + y, x * 4 + (1 - h) * 2 + c)
    direct = second | (z < ZN // 2)
    hub = first & (z == ZN // 2 - 1)

    special = first & (y == 0) & (x == 0) & (c == 0)
    beyond = special & (z >= ZN // 2)
    origin = special & (z == 0)
    relay = special & (z == 1)

    turned = jnp.where(z < ZN // 2, ZN - 1 - z, z)

    def line_at(i):
        place = i + (i >= turned).astype(jnp.int32)
        return jnp.where(z < ZN // 2, ZN - 1 - place, place)

    def signal(sem, peer):
        pl.semaphore_signal(sem, inc=1, device_id=peer, device_id_type=MESH)

    smalls = [
        pltpu.make_async_copy(trace_hbm, trace_ref, lsem.at[4]),
        pltpu.make_async_copy(perm_hbm, perm_ref, lsem.at[5]),
        pltpu.make_async_copy(neigh_hbm, neigh_ref, lsem.at[6]),
        pltpu.make_async_copy(farl_hbm, farl_ref, lsem.at[7]),
        pltpu.make_async_copy(live_hbm, live_ref, lsem.at[8]),
    ]
    for load in smalls:
        load.start()

    barrier = pltpu.get_barrier_semaphore()
    side_peers = [y_peer(k) for k in range(1, YN)] + [e_peer(k) for k in range(1, 8)]
    for i in range(ZN - 1):
        at = line_at(i)

        @pl.when(second | ((at > z) & jnp.logical_not(origin & (at >= ZN // 2))))
        def _():
            signal(barrier, line_peer(at))

    @pl.when(direct)
    def _():
        for peer in side_peers:
            signal(barrier, peer)

    @pl.when(first & is_end)
    def _():
        signal(barrier, touching)

    loads = [
        pltpu.make_async_copy(stiff_hbm, stiff_v, lsem.at[0]),
        pltpu.make_async_copy(exc_hbm, exc_v, lsem.at[1]),
        pltpu.make_async_copy(basis_hbm, basis_v, lsem.at[2]),
        pltpu.make_async_copy(far_hbm, far_v, lsem.at[3]),
    ]
    for load in loads:
        load.start()
    for load in smalls:
        load.wait()

    own = jnp.concatenate([trace_ref[:, q * PATCH : (q + 1) * PATCH] for q in range(QN)], axis=0)
    high, low = split2(own)
    own_hi[...] = high
    own_lo[...] = low
    rows_hi[z] = high
    rows_lo[z] = low
    tab_v[0, 0:4, :] = perm_ref[0]
    for j in range(NB):
        tab_v[0, 4 + j : 5 + j, :] = jnp.full((1, PATCH), neigh_ref[0, j], jnp.int32)
    for f in range(FAR):
        tab_v[0, 8 + f : 9 + f, :] = jnp.full((1, PATCH), farl_ref[0, f], jnp.int32)
    tab_v[0, 10:16, :] = jnp.zeros((6, PATCH), jnp.int32)
    live = live_ref[0]
    centre, steps = cheb_constants()

    def remote(src, dst, send, recv, peer):
        return pltpu.make_async_remote_copy(
            src_ref=src,
            dst_ref=dst,
            send_sem=send,
            recv_sem=recv,
            device_id=peer,
            device_id_type=MESH,
        )

    def z_start(own_ref, rows_ref, part, chosen):
        for i in range(ZN - 1):
            at = line_at(i)

            @pl.when(chosen(at))
            def _():
                remote(
                    own_ref, rows_ref.at[z], zs.at[part, at], zr.at[part, z], line_peer(at)
                ).start()

    def z_wait(own_ref, rows_ref, part, chosen):
        for i in range(ZN - 1):
            at = line_at(i)

            @pl.when(chosen(at))
            def _():
                remote(
                    own_ref, rows_ref.at[at], zs.at[part, at], zr.at[part, at], line_peer(at)
                ).wait_recv()

    def z_sent(own_ref, rows_ref, part, chosen):
        for i in range(ZN - 1):
            at = line_at(i)

            @pl.when(chosen(at))
            def _():
                remote(
                    own_ref, rows_ref.at[z], zs.at[part, at], zr.at[part, z], line_peer(at)
                ).wait_send()

    t_copies = [
        remote(tab_v.at[0], tab_v.at[YN - k], ts.at[k], tr.at[k], y_peer(k)) for k in range(1, YN)
    ]

    def reaches(at):
        return jnp.logical_not(beyond & (at == 0))

    half_rows = rows_hi.at[ZN // 2 : ZN]
    passed = remote(half_rows, half_rows, hs.at[0], hr.at[0], (jnp.where(relay, 0, 1) * YN + y, sub))

    def meet_and_send():
        expected = jnp.where(second, ZN - 1, z - beyond.astype(jnp.int32)) + len(side_peers) * direct.astype(jnp.int32)
        pl.semaphore_wait(barrier, expected + (second & is_end).astype(jnp.int32))

        @pl.when(second & is_end)
        def _():
            for k in range(1, 8):
                signal(side_sem, e_peer(k))

        z_start(own_hi, rows_hi, 0, lambda at: second | ((at < z) & reaches(at)))
        for i in range(ZN - 1):
            at = line_at(i)

            @pl.when(first & (at < z) & reaches(at))
            def _():
                signal(up_sem, line_peer(at))

        @pl.when(direct)
        def _():
            for copy in t_copies:
                copy.start()

        @pl.when(second & is_end)
        def _():
            pl.semaphore_wait(side_sem, 7)
            signal(ready_sem, touching)

    def answer_line():
        @pl.when(z < ZN - 1)
        def _():
            pl.semaphore_wait(up_sem, jnp.where(origin, ZN // 2 - 1, ZN - 1 - z))

        @pl.when(relay)
        def _():
            z_wait(own_hi, rows_hi, 0, lambda at: at >= ZN // 2)
            passed.start()

        @pl.when(origin)
        def _():
            z_start(own_hi, rows_hi, 0, lambda at: (at > z) & (at < ZN // 2))
            passed.wait_recv()

        @pl.when(z == 0)
        def _():
            for k in range(1, 8):
                signal(side_sem, e_peer(k))

        @pl.when(hub)
        def _():
            for peer in side_peers:
                signal(side_sem, peer)

        z_start(own_hi, rows_hi, 0, lambda at: (at > z) & jnp.logical_not(origin & (at < ZN // 2)))

        @pl.when(hub)
        def _():
            pl.semaphore_wait(side_sem, len(side_peers))
            for at in range(ZN // 2, ZN):
                signal(hub_sem, line_peer(at))

    def pass_on():
        for k in range(1, 8):
            signal(ready_sem, line_peer(jnp.where(z == 0, k, ZN - 1 - k)))

    def return_word():
        pl.semaphore_wait(ready_sem, 1)
        signal(ready_sem, touching)
        pass_on()

    def local_work():
        smooth_part()
        prepare_part()

    def smooth_part():
        loads[0].wait()
        row = iota((BLK, BLK), 0)
        col = iota((BLK, BLK), 1)
        operator = stiff_v[0] + jnp.where((row == col) & (row < TROW), robin_gain, 0.0)
        a_high, a_low = split2(operator)
        a3[:, 0:BLK] = a_high
        a3[:, BLK : 2 * BLK] = a_low
        a3[:, 2 * BLK : 3 * BLK] = a_high

        loads[1].wait()
        column = sub * COLS + iota((BLK, COLS), 1)
        r_v[:, 0:COLS] = jnp.where(column < live, exc_v[0].astype(F32), 0.0)
        r_v[:, COLS:] = jnp.where(iota((BLK, PATCH), 0) == iota((BLK, PATCH), 1) % TROW, 1.0, 0.0)
        first = r_v[...] * (1.0 / centre)
        u_v[...] = first
        x_v[...] = first

        def smooth(step, carry):
            u_high, u_low = split2(u_v[...])
            moved = jnp.dot(
                a3[...],
                jnp.concatenate([u_high, u_high, u_low], axis=0),
                preferred_element_type=F32,
            )
            res = r_v[...] - moved
            r_v[...] = res
            keep, add = steps[0]
            for at in range(1, DEG - 1):
                keep = jnp.where(step == at, steps[at][0], keep)
                add = jnp.where(step == at, steps[at][1], add)
            following = keep * u_v[...] + add * res
            u_v[...] = following
            x_v[...] += following
            return carry

        lax.fori_loop(0, DEG - 1, smooth, 0)

    lane = iota((PATCH, PATCH), 1)
    sublane = iota((PATCH, PATCH), 0)

    def prepare_part():
        loads[2].wait()
        for r in range(OWN):
            basis_d[r] = basis_v[0, r : r + 1, :].astype(F32).reshape(256, PATCH)

        g_high, g_low = split2(x_v[:, COLS:])
        g3_v[:, 0:PATCH] = g_high
        g3_v[:, PATCH : 2 * PATCH] = g_high
        g3_v[:, 2 * PATCH :] = g_low
        tiled = jnp.concatenate([x_v[0:TROW, COLS:]] * QN, axis=0)
        gain = jnp.where(lane // TROW == sublane // TROW, (2.0 * robin_gain) * tiled, 0.0)
        b_high, b_low = split2(gain)
        b3_v[:, 0:PATCH] = b_high
        b3_v[:, PATCH : 2 * PATCH] = b_high
        b3_v[:, 2 * PATCH :] = b_low

        pieces = split3((2.0 * robin_gain) * x_v[0:TROW, 0:COLS])
        stacked = jnp.concatenate([piece.astype(F32) for piece in pieces], axis=0).astype(BF16)
        spread = iota((COLS, PATCH), 1) // TROW
        place = iota((COLS, PATCH), 0)
        keep = iota((TROW, PATCH), 0) == iota((TROW, PATCH), 1) % TROW
        for q in range(QN):
            pick = jnp.where(place == q * 16 + spread, 1.0, 0.0).astype(BF16)
            got = jnp.dot(stacked, pick, preferred_element_type=F32)
            got = got[0:8] + got[8:16] + got[16:24]
            t0_v[q : q + 1, :] = jnp.sum(jnp.where(keep, got, 0.0), axis=0, keepdims=True)

    sends_first = first | ((z >= ZN // 4) & (z < ZN - ZN // 4))
    def phase(at, carry):
        @pl.when((at == 0) == sends_first)
        def _():
            meet_and_send()

        @pl.when(at == 0)
        def _():
            local_work()

        return carry

    lax.fori_loop(0, 2, phase, 0)

    @pl.when(first)
    def _():
        answer_line()

    @pl.when(jnp.logical_not(direct))
    def _():
        pl.semaphore_wait(hub_sem, 1)
        for copy in t_copies:
            copy.start()

    @pl.when(first & (z == ZN - 1))
    def _():
        return_word()

    @pl.when(second & is_end)
    def _():
        pl.semaphore_wait(ready_sem, 1)
        pass_on()

    for copy in t_copies:
        copy.wait_recv()
    for t in range(YN):
        for j in range(NB):
            hit = tab_v[t, j : j + 1, :] == sublane
            sel_v[t, j * PATCH : (j + 1) * PATCH, :] = jnp.where(hit, 1.0, 0.0).astype(BF16)

    loads[3].wait()
    z_wait(own_hi, rows_hi, 0, lambda at: jnp.logical_not((relay | origin) & (at >= ZN // 2)))

    def pick_row(t, entry, rows):
        wanted = jnp.broadcast_to(tab_v[t, entry : entry + 1, :], (QN, PATCH))
        found = jnp.zeros((QN, PATCH), F32)
        for k in range(ZN):
            found = jnp.where(wanted == k * YN + y, rows[k], found)
        return found

    f_copies = []
    high_rows = [rows_hi[k].astype(F32) for k in range(ZN)]
    for t in (2, 1, 3, 0):
        for f in range(FAR):
            fsend[t, f] = pick_row(t, 8 + f, high_rows).astype(BF16)
        if t:
            copy = remote(fsend.at[t], frecv.at[t], fs.at[t], fr.at[t], y_peer(t))
            copy.start()
            f_copies.append(copy)
    @pl.when(first & (z == 0))
    def _():
        pl.semaphore_wait(side_sem, 7)
        return_word()


    for copy in f_copies:
        copy.wait_recv()
    partial = jnp.zeros((8, RANK), F32)
    for f in range(FAR):
        remote_rows = fsend[0, f].astype(F32)
        for t in range(1, YN):
            remote_rows += frecv[t, f].astype(F32)
        flat = jnp.concatenate([remote_rows[q : q + 1, :] for q in range(QN)], axis=1)
        flat = jnp.broadcast_to(flat, (8, QN * PATCH)).astype(BF16)
        partial += dot_nt(flat, far_v[0, f])
    csend[:, 0:RANK] = partial[0:1, :]
    csend[:, RANK:] = jnp.zeros((1, 256 - RANK), F32)
    crecv[0] = csend[...]

    @pl.when(jnp.logical_not(is_end))
    def _():
        pl.semaphore_wait(ready_sem, 1)

    c_copies = []
    for dh in (1, 0):
        for dx in (2, 1, 3, 0):
            for dc in (0, 1):
                at = dh * 8 + dx * 2 + dc
                if at:
                    copy = remote(csend, crecv.at[at], cs.at[at], cr.at[at], s_peer(dx, dh, dc))
                    copy.start()
                    c_copies.append(copy)
    z_start(own_lo, rows_lo, 1, lambda at: at >= 0)
    for copy in c_copies:
        copy.wait_recv()

    total = crecv[0]
    for k in range(1, SUB):
        total += crecv[k]
    total = total.astype(BF16).astype(F32)
    mine = iota((16, 256), 1) == sub * OWN + iota((16, 256), 0)
    shares = jnp.sum(jnp.where(mine, jnp.broadcast_to(total, (16, 256)), 0.0), axis=1, keepdims=True)
    weights = [jnp.broadcast_to(shares[r : r + 1, :], (QN, PATCH)) for r in range(OWN)]
    for xx in range(XN):
        for hh in range(2):
            for cc in range(2):
                at = (xx * 4 + hh * 2 + cc) * QN
                value = weights[0] * basis_d[0, at : at + QN, :]
                for r in range(1, OWN):
                    value += weights[r] * basis_d[r, at : at + QN, :]
                psend[hh, xx * 2 + cc] = value
    psend_b[...] = psend[1 - h].astype(BF16)
    p_copies = [[], []]
    for k in (4, 5, 3, 2, 6, 1, 7, 0):
        at = (s8 + k) % 8
        peer = (dom, (at // 2) * 4 + (1 - h) * 2 + at % 2)
        copy = remote(psend_b.at[at], precv_b.at[k], ps.at[0, k], pr.at[0, k], peer)
        copy.start()
        p_copies[0].append(copy)
    for k in range(1, 8):
        copy = remote(psend.at[h, (s8 + k) % 8], precv.at[k], ps.at[1, k], pr.at[1, k], e_peer(k))
        copy.start()
        p_copies[1].append(copy)

    z_wait(own_lo, rows_lo, 1, lambda at: at >= 0)
    full_rows = [rows_hi[k].astype(F32) + rows_lo[k].astype(F32) for k in range(ZN)]
    n_copies = []
    for t in (2, 1, 3, 0):
        faces = jnp.concatenate([pick_row(t, 4 + j, full_rows) for j in range(NB)], axis=1)
        got = jnp.dot(
            jnp.concatenate(split2(faces), axis=0), sel_v[t], preferred_element_type=F32
        )
        nsend[t] = got[0:QN] + got[QN:]
        if t:
            copy = remote(nsend.at[t], nrecv.at[t], ns.at[t], nr.at[t], y_peer(t))
            copy.start()
            n_copies.append(copy)

    for copy in n_copies:
        copy.wait_recv()
    near = (nsend[0] + nrecv[1]) + (nrecv[2] + nrecv[3])
    for copy in p_copies[1]:
        copy.wait_recv()
    far = psend[h, s8]
    for k in range(1, 8):
        far += precv[k]
    for copy in p_copies[0]:
        copy.wait_recv()
    for k in range(8):
        far += precv_b[k].astype(F32)
    incoming = near + far

    patch_col = sub * COLS + iota((QN, PATCH), 0) * 16 + iota((QN, PATCH), 1) // TROW
    live_trace = patch_col < live
    incoming = jnp.where(live_trace, incoming, 0.0)
    i_high, i_low = split2(incoming)
    i3 = jnp.concatenate([i_high, i_low, i_high], axis=1)
    outgoing = t0_v[...] + dot_nt(i3, b3_v[...]) - incoming
    outgoing = jnp.where(live_trace, outgoing, 0.0)
    for q in range(QN):
        next_ref[:, q * PATCH : (q + 1) * PATCH] = outgoing[q : q + 1, :]

    lanes3 = (iota((16, 3 * PATCH), 1) % PATCH) // TROW == iota((16, 3 * PATCH), 0)
    i3f = i3.astype(F32)
    wide = jnp.concatenate(
        [
            jnp.where(lanes3, jnp.broadcast_to(i3f[q : q + 1, :], (16, 3 * PATCH)), 0.0)
            for q in range(QN)
        ],
        axis=0,
    ).astype(BF16)
    field_ref[0] = x_v[:, 0:COLS] + dot_nt(g3_v[...], wide)

    z_sent(own_hi, rows_hi, 0, reaches)

    @pl.when(relay)
    def _():
        passed.wait_send()

    z_sent(own_lo, rows_lo, 1, lambda at: at >= 0)
    for copy in t_copies + f_copies + n_copies + c_copies + p_copies[0] + p_copies[1]:
        copy.wait_send()


def body(*operands):
    vmem = pl.BlockSpec(memory_space=pltpu.VMEM)
    hbm = pl.BlockSpec(memory_space=pltpu.HBM)
    dma = pltpu.SemaphoreType.DMA
    patches = (QN, PATCH)
    return pl.pallas_call(
        kernel,
        out_shape=(
            jax.ShapeDtypeStruct((1, BLK, COLS), F32),
            jax.ShapeDtypeStruct((1, QN * PATCH), F32),
        ),
        in_specs=[hbm] * 9,
        out_specs=(vmem, vmem),
        scratch_shapes=[
            pltpu.VMEM((1, QN * PATCH), F32),
            pltpu.SMEM((1, NB), jnp.int32),
            pltpu.SMEM((1, FAR), jnp.int32),
            pltpu.VMEM((1, NB, PATCH), jnp.int32),
            pltpu.SMEM((1,), jnp.int32),
            pltpu.VMEM((1, BLK, COLS), BF16),
            pltpu.VMEM((1, BLK, BLK), F32),
            pltpu.VMEM((1, FAR, RANK, QN * PATCH), BF16),
            pltpu.VMEM((1, OWN, SUB * QN * PATCH), BF16),
            pltpu.VMEM((OWN, SUB * QN, PATCH), F32),
            pltpu.VMEM((BLK, 3 * BLK), BF16),
            pltpu.VMEM((BLK, VCOLS), F32),
            pltpu.VMEM((BLK, VCOLS), F32),
            pltpu.VMEM((BLK, VCOLS), F32),
            pltpu.VMEM(patches, BF16),
            pltpu.VMEM(patches, BF16),
            pltpu.VMEM((ZN,) + patches, BF16),
            pltpu.VMEM((ZN,) + patches, BF16),
            pltpu.VMEM((YN, 16, PATCH), jnp.int32),
            pltpu.VMEM((YN, NB * PATCH, PATCH), BF16),
            pltpu.VMEM((YN, FAR) + patches, BF16),
            pltpu.VMEM((YN, FAR) + patches, BF16),
            pltpu.VMEM((YN,) + patches, F32),
            pltpu.VMEM((YN,) + patches, F32),
            pltpu.VMEM((1, 256), F32),
            pltpu.VMEM((SUB, 1, 256), F32),
            pltpu.VMEM((2, 8) + patches, F32),
            pltpu.VMEM((8,) + patches, F32),
            pltpu.VMEM((8,) + patches, BF16),
            pltpu.VMEM((8,) + patches, BF16),
            pltpu.VMEM(patches, F32),
            pltpu.VMEM((BLK, 3 * PATCH), BF16),
            pltpu.VMEM((PATCH, 3 * PATCH), BF16),
            dma((9,)),
            dma((2, ZN)),
            dma((2, ZN)),
            dma((YN,)),
            dma((YN,)),
            dma((YN,)),
            dma((YN,)),
            dma((YN,)),
            dma((YN,)),
            dma((SUB,)),
            dma((SUB,)),
            dma((2, 8)),
            dma((2, 8)),
            dma((1,)),
            dma((1,)),
            pltpu.SemaphoreType.REGULAR,
            pltpu.SemaphoreType.REGULAR,
            pltpu.SemaphoreType.REGULAR,
            pltpu.SemaphoreType.REGULAR,
        ],
        name="robin_sweep",
        compiler_params=pltpu.CompilerParams(
            collective_id=0, has_side_effects=True, vmem_limit_bytes=40 * 1024 * 1024
        ),
    )(*[o if o.ndim == 1 else pltpu.with_memory_space_constraint(o, pltpu.HBM) for o in operands])


def solution(mesh):
    placed = (
        P("dom", None, "sub"),
        P("dom", None, None),
        P("dom", "sub"),
        P("dom", None),
        P("dom", None),
        P("dom", None, None),
        P("dom"),
        P("dom", None, None, "sub"),
        P("dom", "sub", None),
    )
    return jax.shard_map(
        body,
        mesh=mesh,
        in_specs=placed,
        out_specs=(P("dom", None, "sub"), P("dom", "sub")),
        check_vma=False,
    )
```
